512 devices in a mesh: stream: 16 (over x_lo, z), cross: 32 (over y, x_hi, core).
Axes of the slice: x: 4 (x_hi: 2, x_lo: 2; x = x_hi * 2 + x_lo), y: 8, z: 8, core: 2. Of those that a mesh axis runs over, the one named last changes fastest.
Arguments:
- state_field: float32 [5, 64, 256, 512], P(None, 'stream', 'cross'), may hold values from -0.6 to 4, as said below
- diag_inverse: float32 [25, 64, 256, 512], P(None, 'stream', 'cross'), may hold values from -0.08 to 1.3, as said below
- boundary_low: int32 [64, 512], P('stream'), may hold values from 0 to 2
- boundary_high: int32 [64, 512], P('stream'), may hold values from 0 to 2
Outputs:
- residual: float32 [5, 64, 256, 512], P(None, 'stream', 'cross')
- update: float32 [5, 64, 256, 512], P(None, 'stream', 'cross')
The draws below stay inside these ranges and needn't reach their ends.
Inputs may be any that keep to these rules, and one draw needn't show every extreme that they name: `boundary_low`: entries of 0 mean slip walls, 1 extrapolation, 2 free stream. `boundary_high`: entries of 0 mean slip walls, 1 extrapolation, 2 free stream. `state_field`: density lies between 0.7 and 1.4, streamwise velocity between -0.05 and 0.05, the other velocities between -0.4 and 0.4, pressure between 0.6 and 1.4. `diag_inverse`: entries on each block's diagonal are positive.
All inputs are finite; a program needn't handle non-finite values.
Results may differ from the reference program's by a relative error of at most 0.0003.
Values sent between devices are 32-bit elements; how exact they have to be, the bound alone decides.
A program may use at most 64 MiB of HBM per device.

```python
import jax
import jax.numpy as jnp
from jax import lax

CK = 512
STREAM_CELLS = 64
NJ = 256


def flow_fields(key, smooth_part, rough_dens, rough_speed, rough_pres):
    key = jax.random.fold_in(key, 21)
    random_key_list = jax.random.split(key, 5)
    shape = (STREAM_CELLS, NJ, CK)
    position = jnp.arange(STREAM_CELLS, dtype=jnp.float32)[:, None, None] * (6.2832 / STREAM_CELLS) + jnp.arange(NJ, dtype=jnp.float32)[None, :, None] * (3.1416 / NJ)
    density = 1.05 + smooth_part * 0.2 * jnp.sin(position) + jax.random.uniform(random_key_list[0], shape, jnp.float32, -rough_dens, rough_dens)
    speed = jax.random.uniform(random_key_list[1], shape, jnp.float32, -rough_speed, rough_speed)
    pressure = 1.0 + smooth_part * 0.2 * jnp.sin(position + 1.0) + jax.random.uniform(random_key_list[2], shape, jnp.float32, -rough_pres, rough_pres)
    side_speed = jax.random.uniform(random_key_list[3], shape, jnp.float32, -0.4, 0.4)
    span_speed = jax.random.uniform(random_key_list[4], shape, jnp.float32, -0.4, 0.4)
    return (density, speed, side_speed, span_speed, pressure)


def draw_state_field(key, part):
    flow = flow_fields(key, 0.0, 0.25, 0.05, 0.3)
    density, speed, side_speed, span_speed, pressure = flow
    energy = pressure / 0.4 + 0.5 * density * (speed * speed + side_speed * side_speed + span_speed * span_speed)
    return jnp.stack([density, density * speed, density * side_speed, density * span_speed, energy])


def draw_diag_inverse(key, part):
    flow = flow_fields(key, 0.0, 0.25, 0.05, 0.3)
    lowest_ratio = 0.95
    key = jax.random.fold_in(key, 12)
    random_key_list = jax.random.split(key, 3)
    density, speed, side_speed, span_speed, pressure = flow
    largest_eigenvalue = jnp.abs(speed) + jnp.sqrt(1.4 * pressure / density)
    courant_number = jax.random.uniform(random_key_list[0], (STREAM_CELLS, NJ, CK), jnp.float32, lowest_ratio, 0.995)
    surge_plane_list = jax.random.randint(random_key_list[1], (2,), 0, STREAM_CELLS)
    plane_numbers = jnp.arange(STREAM_CELLS)[:, None, None]
    surge_flag = jnp.any(plane_numbers[None] == surge_plane_list[:, None, None, None], axis=0)
    surge_multiplier = jnp.where(surge_flag, 0.7, 1.0)
    diagonal_factor = courant_number * surge_multiplier / largest_eigenvalue
    others = jax.random.uniform(random_key_list[2], (25, STREAM_CELLS, NJ, CK), jnp.float32, -0.06, 0.06)
    on_diagonal = (jnp.arange(25) % 6 == 0)[:, None, None, None]
    return jnp.where(on_diagonal, 1.0, others) * diagonal_factor[None]


def with_ends(values, own_key, low, largest):
    index_at = [jax.random.randint(jax.random.fold_in(own_key, axis), (), 0, length) for axis, length in enumerate(values.shape)]
    widest = values.shape.index(max(values.shape))
    neighbour = index_at[:widest] + [(index_at[widest] + 1) % values.shape[widest]] + index_at[widest + 1:]
    return values.at[tuple(index_at)].set(low).at[tuple(neighbour)].set(largest)


def setup_inputs(seed: int = 0) -> dict:
    splits = jax.random.split(jax.random.key(seed), 5)
    return {
        "state_field": draw_state_field(jax.random.fold_in(splits[4], 71), 0),
        "diag_inverse": draw_diag_inverse(jax.random.fold_in(splits[4], 71), 0),
        "boundary_low": with_ends(jax.random.randint(splits[2], (STREAM_CELLS, CK), 0, 3), jax.random.fold_in(splits[2], 1), 0, 2).astype(jnp.int32),
        "boundary_high": with_ends(jax.random.randint(splits[3], (STREAM_CELLS, CK), 0, 3), jax.random.fold_in(splits[3], 1), 0, 2).astype(jnp.int32),
    }


gas_gamma = 1.4
free_values = (1.0, 0.0, 0.0, 0.0, 2.5)

def primitive(conserved):
    density = conserved[0]
    velocity = [conserved[1] / density, conserved[2] / density, conserved[3] / density]
    kinetic = conserved[1] * velocity[0] + conserved[2] * velocity[1] + conserved[3] * velocity[2]
    pressure = (gas_gamma - 1.0) * (conserved[4] - 0.5 * kinetic)
    return (density, velocity, pressure)

def euler_flux(conserved, direction):
    density, velocity, pressure = primitive(conserved)
    normal = velocity[direction]
    pieces = [conserved[0] * normal, conserved[1] * normal, conserved[2] * normal, conserved[3] * normal, (conserved[4] + pressure) * normal]
    pieces[1 + direction] = pieces[1 + direction] + pressure
    return jnp.stack(pieces)

def roe_flux(left_state, right_state, direction):
    left_dens, left_vel, left_pres = primitive(left_state)
    right_dens, right_vel, right_pres = primitive(right_state)
    left_enth = (left_state[4] + left_pres) / left_dens
    right_enth = (right_state[4] + right_pres) / right_dens
    left_root = jnp.sqrt(left_dens)
    right_root = jnp.sqrt(right_dens)
    root_total = left_root + right_root
    average_vel = [(left_root * left_vel[component] + right_root * right_vel[component]) / root_total for component in range(3)]
    average_enth = (left_root * left_enth + right_root * right_enth) / root_total
    kinetic = 0.5 * (average_vel[0] * average_vel[0] + average_vel[1] * average_vel[1] + average_vel[2] * average_vel[2])
    sound_sq = (gas_gamma - 1.0) * (average_enth - kinetic)
    sound = jnp.sqrt(sound_sq)
    average_dens = left_root * right_root
    normal = average_vel[direction]
    jump_dens = right_dens - left_dens
    jump_pres = right_pres - left_pres
    jump_vel = [right_vel[component] - left_vel[component] for component in range(3)]
    jump_normal = jump_vel[direction]
    wave_slow = (jump_pres - average_dens * sound * jump_normal) / (2.0 * sound_sq)
    wave_fast = (jump_pres + average_dens * sound * jump_normal) / (2.0 * sound_sq)
    wave_entropy = jump_dens - jump_pres / sound_sq
    speed_middle = jnp.abs(normal)
    slow_part = jnp.abs(normal - sound) * wave_slow
    fast_part = jnp.abs(normal + sound) * wave_fast
    dissipation = [slow_part + speed_middle * wave_entropy + fast_part]
    for component in range(3):
        unit_normal = 1.0 if component == direction else 0.0
        tangent = jump_vel[component] - unit_normal * jump_normal
        dissipation.append(slow_part * (average_vel[component] - unit_normal * sound) + speed_middle * (wave_entropy * average_vel[component] + average_dens * tangent) + fast_part * (average_vel[component] + unit_normal * sound))
    along_jump = average_vel[0] * jump_vel[0] + average_vel[1] * jump_vel[1] + average_vel[2] * jump_vel[2] - normal * jump_normal
    dissipation.append(slow_part * (average_enth - normal * sound) + speed_middle * (wave_entropy * kinetic + average_dens * along_jump) + fast_part * (average_enth + normal * sound))
    return 0.5 * (euler_flux(left_state, direction) + euler_flux(right_state, direction)) - 0.5 * jnp.stack(dissipation)

def spectral(conserved):
    density, velocity, pressure = primitive(conserved)
    return jnp.abs(velocity[0]) + jnp.sqrt(gas_gamma * pressure / density)

def jacobian_product(conserved, change):
    return jax.jvp(lambda probe_state: euler_flux(probe_state, 0), (conserved,), (change,))[1]

def lower_term(conserved, change):
    return 0.5 * (jacobian_product(conserved, change) + spectral(conserved) * change)

def upper_term(conserved, change):
    return 0.5 * (jacobian_product(conserved, change) - spectral(conserved) * change)

def apply_inverse(inverse, vector):
    matrix = jnp.reshape(inverse, (5, 5) + inverse.shape[1:])
    return lax.optimization_barrier(jnp.sum(matrix * vector[None], axis=1))

def free_plane(like_state):
    column = jnp.reshape(jnp.array(free_values, like_state.dtype), (5,) + (1,) * (like_state.ndim - 1))
    return column * jnp.ones_like(like_state)

def ghost_state(interior, face_kinds, direction):
    sign_flip = [1.0] * 5
    sign_flip[1 + direction] = -1.0
    mirror = interior * jnp.reshape(jnp.array(sign_flip, interior.dtype), (5,) + (1,) * (interior.ndim - 1))
    return jnp.where(face_kinds[None] == 0, mirror, jnp.where(face_kinds[None] == 1, interior, free_plane(interior)))

def reference(state_field, diag_inverse, boundary_low, boundary_high):
    extended = jnp.concatenate([free_plane(state_field[:, :1]), state_field, state_field[:, -1:]], axis=1)

    def plane_residual(plane_index):
        below = lax.dynamic_index_in_dim(extended, plane_index, 1, keepdims=False)
        centre = lax.dynamic_index_in_dim(extended, plane_index + 1, 1, keepdims=False)
        above = lax.dynamic_index_in_dim(extended, plane_index + 2, 1, keepdims=False)
        low_kinds = lax.dynamic_index_in_dim(boundary_low, plane_index, 0, keepdims=False)
        high_kinds = lax.dynamic_index_in_dim(boundary_high, plane_index, 0, keepdims=False)
        low_side = ghost_state(centre[:, 0], low_kinds, 1)
        high_side = ghost_state(centre[:, -1], high_kinds, 1)
        wide_plane = jnp.concatenate([low_side[:, None], centre, high_side[:, None]], axis=1)
        flux_stream = roe_flux(centre, above, 0) - roe_flux(below, centre, 0)
        faces_cross = roe_flux(wide_plane[:, :-1], wide_plane[:, 1:], 1)
        flux_cross = faces_cross[:, 1:] - faces_cross[:, :-1]
        faces_span = roe_flux(centre, jnp.roll(centre, -1, axis=-1), 2)
        flux_span = faces_span - jnp.roll(faces_span, 1, axis=-1)
        return flux_stream + flux_cross + flux_span
    residual = jnp.moveaxis(lax.map(plane_residual, jnp.arange(STREAM_CELLS)), 0, 1)

    def forward_step(state_pair, plane_index):
        previous, previous_state = state_pair
        current_state = lax.dynamic_index_in_dim(state_field, plane_index, 1, keepdims=False)
        drive = -lax.dynamic_index_in_dim(residual, plane_index, 1, keepdims=False) + lower_term(previous_state, previous)
        current = apply_inverse(lax.dynamic_index_in_dim(diag_inverse, plane_index, 1, keepdims=False), drive)
        return ((current, current_state), current)
    zero_plane = jnp.zeros_like(state_field[:, 0])
    star_planes = lax.scan(forward_step, (zero_plane, state_field[:, 0]), jnp.arange(STREAM_CELLS))[1]
    star = jnp.moveaxis(star_planes, 0, 1)

    def backward_step(state_pair, plane_index):
        following, following_state = state_pair
        current_state = lax.dynamic_index_in_dim(state_field, plane_index, 1, keepdims=False)
        inverse = lax.dynamic_index_in_dim(diag_inverse, plane_index, 1, keepdims=False)
        current = lax.dynamic_index_in_dim(star, plane_index, 1, keepdims=False) - apply_inverse(inverse, upper_term(following_state, following))
        return ((current, current_state), current)
    update_planes = lax.scan(backward_step, (zero_plane, state_field[:, -1]), jnp.arange(STREAM_CELLS), reverse=True)[1]
    return (residual, jnp.moveaxis(update_planes, 0, 1))
```

```python
import functools

import jax
import jax.numpy as jnp
from jax import lax
from jax.experimental import pallas as pl
from jax.experimental.pallas import tpu as pltpu
from jax.sharding import PartitionSpec as P

MESH = pl.DeviceIdType.MESH
free_values = (1.0, 0.0, 0.0, 0.0, 2.5)
CHUNK = 128
RHO, U1, U2, U3, PRES, ENTH, ROOT = range(7)


def primitive(q):
    inv_root = lax.rsqrt(q[0])
    inv = inv_root * inv_root
    u = [q[1] * inv, q[2] * inv, q[3] * inv]
    pressure = 0.4 * (q[4] - 0.5 * (q[1] * u[0] + q[2] * u[1] + q[3] * u[2]))
    return [q[0], *u, pressure, (q[4] + pressure) * inv, q[0] * inv_root]


def roe_twice(left, right, d):
    share = right[ROOT] / (left[ROOT] + right[ROOT])
    jump = [right[1 + k] - left[1 + k] for k in range(3)]
    avg = [left[1 + k] + share * jump[k] for k in range(3)]
    enth = left[ENTH] + share * (right[ENTH] - left[ENTH])
    kinetic = 0.5 * (avg[0] * avg[0] + avg[1] * avg[1] + avg[2] * avg[2])
    sound_sq = 0.4 * (enth - kinetic)
    inv_sound = lax.rsqrt(sound_sq)
    sound = sound_sq * inv_sound
    inv_sq = inv_sound * inv_sound
    dens = left[ROOT] * right[ROOT]
    normal = avg[d]
    scaled_pres = (right[PRES] - left[PRES]) * inv_sq
    scaled_jump = dens * inv_sound * jump[d]
    slow = jnp.abs(normal - sound) * (0.5 * (scaled_pres - scaled_jump))
    fast = jnp.abs(normal + sound) * (0.5 * (scaled_pres + scaled_jump))
    speed = jnp.abs(normal)
    entropy = speed * (right[RHO] - left[RHO] - scaled_pres)
    shear = speed * dens
    acoustic = slow + fast
    total = acoustic + entropy
    spread = (fast - slow) * sound
    mass_left = left[RHO] * left[1 + d]
    mass_right = right[RHO] * right[1 + d]
    pieces = [mass_left + mass_right - total]
    along = 0.0
    for k in range(3):
        central = mass_left * left[1 + k] + mass_right * right[1 + k]
        if k == d:
            pieces.append(central + (left[PRES] + right[PRES]) - (total * avg[k] + spread))
        else:
            pieces.append(central - (total * avg[k] + shear * jump[k]))
            along = along + avg[k] * jump[k]
    pieces.append(
        mass_left * left[ENTH]
        + mass_right * right[ENTH]
        - (acoustic * enth + spread * normal + entropy * kinetic + shear * along)
    )
    return pieces


def half_jacobian(w):
    u, v, s = 0.5 * w[U1], 0.5 * w[U2], 0.5 * w[U3]
    phi = 0.1 * (w[U1] * w[U1] + w[U2] * w[U2] + w[U3] * w[U3])
    inv_root = w[ROOT] / w[RHO]
    pos = 1.4 * w[PRES]
    lam = jnp.abs(u) + 0.5 * (pos * lax.rsqrt(pos) * inv_root)
    return u, v, s, phi, 0.5 * w[ENTH], lam, w[U1], w[U2], w[U3]


def row_times(row, jac, sign):
    u, v, s, phi, enth, lam, u1, _, _ = jac
    pres = row[1] + u1 * row[4]
    move = u * row[1] + v * row[2] + s * row[3] + enth * row[4]
    own = u + sign * lam
    return [
        phi * pres - u1 * move + (sign * lam) * row[0],
        0.5 * row[0] + own * row[1] + move - 0.4 * (u * pres),
        own * row[2] - 0.4 * (v * pres),
        own * row[3] - 0.4 * (s * pres),
        own * row[4] + 0.2 * pres,
    ]


def mat_vec(load, vec):
    out = []
    for r in range(5):
        total = load(5 * r) * vec[0]
        for k in range(1, 5):
            total = total + load(5 * r + k) * vec[k]
        out.append(total)
    return out


def kernel(
    streams, crosses,
    state, diag_hbm, kinds_low, kinds_high, res_hbm, upd_hbm,
    diag, prim, edge, halo_cross, halo_stream, low_prim, top_flux,
    flux_stream, res, drive, mats_f, mats_b, prod_f, prod_b, base, upd,
    f_in, f_out, b_in, b_out,
    diag_sem, out_sem, halo_send, halo_recv, f_send, f_recv, b_send, b_recv,
):
    me = lax.axis_index("stream")
    mine = lax.axis_index("cross")
    planes, rows, lanes = state.shape[1:]
    chunks = lanes // CHUNK
    up = {"stream": lax.rem(me + 1, streams)}
    down = {"stream": lax.rem(me + streams - 1, streams)}
    high = {"cross": lax.rem(mine + 1, crosses)}
    low = {"cross": lax.rem(mine + crosses - 1, crosses)}

    load_diag = pltpu.make_async_copy(diag_hbm, diag, diag_sem)
    load_diag.start()
    barrier = pltpu.get_barrier_semaphore()
    for to in (up, down, high, low):
        pl.semaphore_signal(barrier, inc=1, device_id=to, device_id_type=MESH)

    for p in range(planes):
        for k in range(5):
            edge[0, k, pl.ds(p, 1), :] = state[k, p, pl.ds(0, 1), :]
            edge[1, k, pl.ds(p, 1), :] = state[k, p, pl.ds(rows - 1, 1), :]
    pl.semaphore_wait(barrier, 4)

    def remote(src, dst, send, recv, to):
        return pltpu.make_async_remote_copy(
            src_ref=src, dst_ref=dst, send_sem=send, recv_sem=recv,
            device_id=to, device_id_type=MESH,
        )

    halos = [
        remote(edge.at[1], halo_cross.at[0], halo_send.at[0], halo_recv.at[0], high),
        remote(edge.at[0], halo_cross.at[1], halo_send.at[1], halo_recv.at[1], low),
        remote(state.at[:, planes - 1], halo_stream.at[0], halo_send.at[2], halo_recv.at[2], up),
        remote(state.at[:, 0], halo_stream.at[1], halo_send.at[3], halo_recv.at[3], down),
    ]
    for copy in halos:
        copy.start()

    def get(ref, index, count):
        return [ref[(k, *index)] for k in range(count)]

    def put(ref, index, values):
        for k, value in enumerate(values):
            ref[(k, *index)] = value

    def own_plane(p, carry):
        cell = primitive(get(state, (p,), 5))
        put(prim, (p + 1,), cell)
        ahead = [pltpu.roll(field, lanes - 1, 1) for field in cell]
        face = roe_twice(cell, ahead, 2)
        put(res, (p,), [f - pltpu.roll(f, 1, 1) for f in face])
        return carry

    lax.fori_loop(0, planes, own_plane, 0)

    def inner_face(f, carry):
        put(flux_stream, (f,), roe_twice(get(prim, (f,), 7), get(prim, (f + 1,), 7), 0))
        return carry

    lax.fori_loop(1, planes, inner_face, 0)

    for copy in halos:
        copy.wait()

    below = [
        jnp.where(me == 0, free_values[k], halo_stream[0, k]) for k in range(5)
    ]
    put(prim, (0,), primitive(below))
    above = [
        jnp.where(me == streams - 1, state[k, planes - 1], halo_stream[1, k]) for k in range(5)
    ]
    put(prim, (planes + 1,), primitive(above))
    lax.fori_loop(0, 2, lambda i, c: inner_face(i * planes, c), 0)

    def ghost(cell, kinds):
        out = []
        for k in range(5):
            mirror = -cell[k] if k == 2 else cell[k]
            out.append(
                jnp.where(kinds == 0, mirror, jnp.where(kinds == 1, cell[k], free_values[k]))
            )
        return out

    first = [edge[0, k] for k in range(5)]
    last = [edge[1, k] for k in range(5)]
    ghost_low = ghost(first, kinds_low[...])
    ghost_high = ghost(last, kinds_high[...])
    side_low = [jnp.where(mine == 0, ghost_low[k], halo_cross[0, k]) for k in range(5)]
    side_high = [
        jnp.where(mine == crosses - 1, ghost_high[k], halo_cross[1, k]) for k in range(5)
    ]
    put(low_prim, (), primitive(side_low))
    put(top_flux, (), roe_twice(primitive(last), primitive(side_high), 1))

    load_diag.wait()
    row_no = lax.broadcasted_iota(jnp.int32, (rows, lanes), 0)

    def plane_residual(p, previous):
        cell = get(prim, (p + 1,), 7)
        under = [
            jnp.where(row_no == 0, low_prim[k, pl.ds(p, 1), :], pltpu.roll(cell[k], 1, 0))
            for k in range(7)
        ]
        face = roe_twice(under, cell, 1)
        total = []
        for k in range(5):
            over = jnp.where(
                row_no == rows - 1,
                top_flux[k, pl.ds(p, 1), :],
                pltpu.roll(face[k], rows - 1, 0),
            )
            total.append(
                0.5
                * (
                    (flux_stream[k, p + 1] - flux_stream[k, p])
                    + (over - face[k])
                    + res[k, p]
                )
            )
        put(res, (p,), total)
        return previous

    lax.fori_loop(0, planes, plane_residual, 0)
    save_res = pltpu.make_async_copy(res, res_hbm, out_sem.at[0])
    save_res.start()

    def plane_drive(p, previous):
        jac = half_jacobian(get(prim, (p,), 7))
        u, v, s, phi, enth, lam, u1, _, _ = jac
        own = u + lam
        q = previous[1] - u1 * previous[0]
        pres = (
            phi * previous[0]
            - 0.4 * (u * previous[1] + v * previous[2] + s * previous[3])
            + 0.2 * previous[4]
        )
        term = [
            0.5 * previous[1] + lam * previous[0],
            own * previous[1] + u * q + pres,
            own * previous[2] + v * q,
            own * previous[3] + s * q,
            own * previous[4] + u1 * pres + enth * q,
        ]
        vec = [term[k] - res[k, p] for k in range(5)]
        out = mat_vec(lambda e: diag[e, p], vec)
        put(drive, (p,), out)
        return tuple(out)

    zero = jnp.zeros((rows, lanes), jnp.float32)
    lax.fori_loop(0, planes, plane_drive, (zero,) * 5)

    def spot(c):
        return pl.ds(pl.multiple_of(c * CHUNK, CHUNK), CHUNK)

    def f_copy(c):
        return remote(f_out.at[c], f_in.at[c], f_send.at[c], f_recv.at[c], up)

    def b_copy(c):
        return remote(b_out.at[c], b_in.at[c], b_send.at[c], b_recv.at[c], down)

    @pl.when(me == 0)
    def _():
        def start(c, carry):
            for k in range(5):
                f_out[c, k] = drive[k, planes - 1, :, spot(c)]
            f_copy(c).start()
            return carry

        lax.fori_loop(0, chunks, start, 0)

    def matrices(p, carry):
        jac_low = half_jacobian(get(prim, (p,), 7))
        jac_high = half_jacobian(get(prim, (p + 2,), 7))
        for r in range(5):
            row = [diag[5 * r + k, p] for k in range(5)]
            for k, value in enumerate(row_times(row, jac_low, 1.0)):
                mats_f[5 * r + k, p] = value
            minus = [-value for value in row]
            for k, value in enumerate(row_times(minus, jac_high, -1.0)):
                mats_b[5 * r + k, p] = value
        return carry

    lax.fori_loop(0, planes, matrices, 0)

    def multiply(mats, prod, p):
        def column(j, carry):
            vec = [prod[5 * k + j] for k in range(5)]
            for r, value in enumerate(mat_vec(lambda e: mats[e, p], vec)):
                prod[5 * r + j] = value
            return carry

        lax.fori_loop(0, 5, column, 0)

    def start_product(mats, prod, p):
        def entry(e, carry):
            prod[e] = mats[e, p]
            return carry

        lax.fori_loop(0, 25, entry, 0)

    start_product(mats_f, prod_f, 0)
    lax.fori_loop(1, planes, lambda p, c: (multiply(mats_f, prod_f, p), c)[1], 0)

    def settle(c):
        at = spot(c)
        delta = [jnp.where(me == 0, 0.0, f_in[c, k]) for k in range(5)]
        star = []
        for p in range(planes):
            delta = mat_vec(lambda e: mats_f[e, p, :, at], delta)
            star.append([drive[k, p, :, at] + delta[k] for k in range(5)])
        current = star[planes - 1]
        for p in reversed(range(planes)):
            if p < planes - 1:
                step = mat_vec(lambda e: mats_b[e, p, :, at], current)
                current = [star[p][k] + step[k] for k in range(5)]
            for k in range(5):
                base[k, p, :, at] = current[k]
        return current

    def f_relay(c, carry):
        f_copy(c).wait_recv()
        at = spot(c)
        step = mat_vec(lambda e: prod_f[e, :, at], [f_in[c, k] for k in range(5)])
        for k in range(5):
            f_out[c, k] = drive[k, planes - 1, :, at] + step[k]
        f_copy(c).start()
        return carry

    @pl.when((me > 0) & (me < streams - 1))
    def _():
        lax.fori_loop(0, chunks, f_relay, 0)

    @pl.when(me < streams - 1)
    def _():
        lax.fori_loop(0, chunks, lambda c, carry: (settle(c), carry)[1], 0)
        start_product(mats_b, prod_b, planes - 1)
        lax.fori_loop(
            1, planes, lambda i, carry: (multiply(mats_b, prod_b, planes - 1 - i), carry)[1], 0
        )

    @pl.when(me == streams - 1)
    def _():
        def turn(c, carry):
            f_copy(c).wait_recv()
            current = settle(c)
            for k in range(5):
                b_out[c, k] = current[k]
            b_copy(c).start()
            return carry

        lax.fori_loop(0, chunks, turn, 0)

    def b_relay(c, carry):
        b_copy(c).wait_recv()
        at = spot(c)
        step = mat_vec(lambda e: prod_b[e, :, at], [b_in[c, k] for k in range(5)])
        for k in range(5):
            b_out[c, k] = base[k, 0, :, at] + step[k]
        b_copy(c).start()
        return carry

    @pl.when((me > 0) & (me < streams - 1))
    def _():
        lax.fori_loop(0, chunks, b_relay, 0)

    def finish(c, carry):
        at = spot(c)
        delta = [jnp.where(me == streams - 1, 0.0, b_in[c, k]) for k in range(5)]
        for p in reversed(range(planes)):
            delta = mat_vec(lambda e: mats_b[e, p, :, at], delta)
            for k in range(5):
                upd[k, p, :, at] = base[k, p, :, at] + delta[k]
        return carry

    @pl.when(me > 0)
    def _():
        lax.fori_loop(0, chunks, finish, 0)

    @pl.when(me == 0)
    def _():
        def last_step(c, carry):
            b_copy(c).wait_recv()
            return finish(c, carry)

        lax.fori_loop(0, chunks, last_step, 0)

    save_upd = pltpu.make_async_copy(upd, upd_hbm, out_sem.at[1])
    save_upd.start()

    @pl.when(me < streams - 1)
    def _():
        lax.fori_loop(0, chunks, lambda c, carry: (f_copy(c).wait_send(), carry)[1], 0)

    @pl.when(me > 0)
    def _():
        lax.fori_loop(0, chunks, lambda c, carry: (b_copy(c).wait_send(), carry)[1], 0)

    save_res.wait()
    save_upd.wait()


def local(streams, crosses, state, diag, kinds_low, kinds_high):
    _, planes, rows, lanes = state.shape
    chunks = lanes // CHUNK
    f32 = jnp.float32
    block = (planes, rows, lanes)

    def vmem(*shape):
        return pltpu.VMEM(shape, f32)

    return pl.pallas_call(
        functools.partial(kernel, streams, crosses),
        out_shape=[jax.ShapeDtypeStruct(state.shape, f32)] * 2,
        in_specs=[
            pl.BlockSpec(memory_space=pltpu.VMEM),
            pl.BlockSpec(memory_space=pl.ANY),
            pl.BlockSpec(memory_space=pltpu.VMEM),
            pl.BlockSpec(memory_space=pltpu.VMEM),
        ],
        out_specs=[pl.BlockSpec(memory_space=pl.ANY)] * 2,
        scratch_shapes=[
            vmem(25, *block),
            vmem(7, planes + 2, rows, lanes),
            vmem(2, 5, planes, lanes),
            vmem(2, 5, planes, lanes),
            vmem(2, 5, rows, lanes),
            vmem(7, planes, lanes),
            vmem(5, planes, lanes),
            vmem(5, planes + 1, rows, lanes),
            vmem(5, *block),
            vmem(5, *block),
            vmem(25, *block),
            vmem(25, *block),
            vmem(25, rows, lanes),
            vmem(25, rows, lanes),
            vmem(5, *block),
            vmem(5, *block),
            vmem(chunks, 5, rows, CHUNK),
            vmem(chunks, 5, rows, CHUNK),
            vmem(chunks, 5, rows, CHUNK),
            vmem(chunks, 5, rows, CHUNK),
            pltpu.SemaphoreType.DMA,
            pltpu.SemaphoreType.DMA((2,)),
            pltpu.SemaphoreType.DMA((4,)),
            pltpu.SemaphoreType.DMA((4,)),
            pltpu.SemaphoreType.DMA((chunks,)),
            pltpu.SemaphoreType.DMA((chunks,)),
            pltpu.SemaphoreType.DMA((chunks,)),
            pltpu.SemaphoreType.DMA((chunks,)),
        ],
        compiler_params=pltpu.CompilerParams(
            collective_id=0, has_side_effects=True, vmem_limit_bytes=40 * 2**20
        ),
        cost_estimate=pl.CostEstimate(
            flops=16000000, bytes_accessed=2700000, transcendentals=100000
        ),
    )(state, diag, kinds_low, kinds_high)


def solution(mesh):
    spec = P(None, "stream", "cross", None)
    return jax.shard_map(
        functools.partial(local, mesh.shape["stream"], mesh.shape["cross"]),
        mesh=mesh,
        in_specs=(spec, spec, P("stream", None), P("stream", None)),
        out_specs=(spec, spec),
        check_vma=False,
    )
```

```python
import functools

import jax
import jax.numpy as jnp
from jax import lax
from jax.experimental import pallas as pl
from jax.experimental.pallas import tpu as pltpu
from jax.sharding import PartitionSpec as P

MESH = pl.DeviceIdType.MESH
free_values = (1.0, 0.0, 0.0, 0.0, 2.5)
CHUNK = 128
RHO, U1, U2, U3, PRES, ENTH, ROOT = range(7)


def primitive(q):
    inv_root = lax.rsqrt(q[0])
    inv = inv_root * inv_root
    u = [q[1] * inv, q[2] * inv, q[3] * inv]
    pressure = 0.4 * (q[4] - 0.5 * (q[1] * u[0] + q[2] * u[1] + q[3] * u[2]))
    return [q[0], *u, pressure, (q[4] + pressure) * inv, q[0] * inv_root]


def roe_twice(left, right, d):
    share = right[ROOT] / (left[ROOT] + right[ROOT])
    jump = [right[1 + k] - left[1 + k] for k in range(3)]
    avg = [left[1 + k] + share * jump[k] for k in range(3)]
    enth = left[ENTH] + share * (right[ENTH] - left[ENTH])
    kinetic = 0.5 * (avg[0] * avg[0] + avg[1] * avg[1] + avg[2] * avg[2])
    sound_sq = 0.4 * (enth - kinetic)
    inv_sound = lax.rsqrt(sound_sq)
    sound = sound_sq * inv_sound
    inv_sq = inv_sound * inv_sound
    dens = left[ROOT] * right[ROOT]
    normal = avg[d]
    scaled_pres = (right[PRES] - left[PRES]) * inv_sq
    scaled_jump = dens * inv_sound * jump[d]
    slow = jnp.abs(normal - sound) * (0.5 * (scaled_pres - scaled_jump))
    fast = jnp.abs(normal + sound) * (0.5 * (scaled_pres + scaled_jump))
    speed = jnp.abs(normal)
    entropy = speed * (right[RHO] - left[RHO] - scaled_pres)
    shear = speed * dens
    acoustic = slow + fast
    total = acoustic + entropy
    spread = (fast - slow) * sound
    mass_left = left[RHO] * left[1 + d]
    mass_right = right[RHO] * right[1 + d]
    pieces = [mass_left + mass_right - total]
    along = 0.0
    for k in range(3):
        central = mass_left * left[1 + k] + mass_right * right[1 + k]
        if k == d:
            pieces.append(central + (left[PRES] + right[PRES]) - (total * avg[k] + spread))
        else:
            pieces.append(central - (total * avg[k] + shear * jump[k]))
            along = along + avg[k] * jump[k]
    pieces.append(
        mass_left * left[ENTH]
        + mass_right * right[ENTH]
        - (acoustic * enth + spread * normal + entropy * kinetic + shear * along)
    )
    return pieces


def half_jacobian(w):
    u, v, s = 0.5 * w[U1], 0.5 * w[U2], 0.5 * w[U3]
    phi = 0.1 * (w[U1] * w[U1] + w[U2] * w[U2] + w[U3] * w[U3])
    inv_root = w[ROOT] / w[RHO]
    pos = 1.4 * w[PRES]
    lam = jnp.abs(u) + 0.5 * (pos * lax.rsqrt(pos) * inv_root)
    return u, v, s, phi, 0.5 * w[ENTH], lam, w[U1], w[U2], w[U3]


def row_times(row, jac, sign):
    u, v, s, phi, enth, lam, u1, _, _ = jac
    pres = row[1] + u1 * row[4]
    move = u * row[1] + v * row[2] + s * row[3] + enth * row[4]
    own = u + sign * lam
    return [
        phi * pres - u1 * move + (sign * lam) * row[0],
        0.5 * row[0] + own * row[1] + move - 0.4 * (u * pres),
        own * row[2] - 0.4 * (v * pres),
        own * row[3] - 0.4 * (s * pres),
        own * row[4] + 0.2 * pres,
    ]


def mat_vec(load, vec):
    out = []
    for r in range(5):
        total = load(5 * r) * vec[0]
        for k in range(1, 5):
            total = total + load(5 * r + k) * vec[k]
        out.append(total)
    return out


def kernel(
    streams, crosses,
    state_hbm, diag_hbm, low_hbm, high_hbm, res_hbm, upd_hbm,
    state, diag, kinds_low, kinds_high, prim, edge, halo_cross, halo_stream, low_prim, top_flux,
    flux_stream, res, drive, mats_f, mats_b, prod, base, upd,
    p_out, p_in, q_out, q_in, a_out, a_in, s_out, s_in, b_out, b_in, u_out, u_in,
    load_sem, save_sem, halo_send, halo_recv, sends, recvs,
):
    me = lax.axis_index("stream")
    mine = lax.axis_index("cross")
    planes, rows, lanes = state.shape[1:]
    chunks = lanes // CHUNK
    piece = rows * chunks // streams
    per_chunk = rows // piece
    last = streams - 1
    up = {"stream": lax.rem(me + 1, streams)}
    down = {"stream": lax.rem(me + last, streams)}
    high = {"cross": lax.rem(mine + 1, crosses)}
    low = {"cross": lax.rem(mine + crosses - 1, crosses)}

    loads = [
        pltpu.make_async_copy(src, dst, load_sem.at[i])
        for i, (src, dst) in enumerate(
            [(state_hbm, state), (diag_hbm, diag), (low_hbm, kinds_low), (high_hbm, kinds_high)]
        )
    ]
    for copy in loads:
        copy.start()
    barrier = pltpu.get_barrier_semaphore()

    def greet(o, carry):
        pl.semaphore_signal(
            barrier, inc=1, device_id={"stream": lax.rem(me + o, streams)}, device_id_type=MESH
        )
        return carry

    lax.fori_loop(1, streams, greet, 0)
    for to in (high, low):
        pl.semaphore_signal(barrier, inc=1, device_id=to, device_id_type=MESH)

    loads[0].wait()
    for p in range(planes):
        for k in range(5):
            edge[0, k, pl.ds(p, 1), :] = state[k, p, pl.ds(0, 1), :]
            edge[1, k, pl.ds(p, 1), :] = state[k, p, pl.ds(rows - 1, 1), :]
    pl.semaphore_wait(barrier, streams + 1)

    def remote(src, dst, send, recv, to):
        return pltpu.make_async_remote_copy(
            src_ref=src, dst_ref=dst, send_sem=send, recv_sem=recv,
            device_id=to, device_id_type=MESH,
        )

    halos = [
        remote(state.at[:, planes - 1], halo_stream.at[0], halo_send.at[0], halo_recv.at[0], up),
        remote(state.at[:, 0], halo_stream.at[1], halo_send.at[1], halo_recv.at[1], down),
        remote(edge.at[1], halo_cross.at[0], halo_send.at[2], halo_recv.at[2], high),
        remote(edge.at[0], halo_cross.at[1], halo_send.at[3], halo_recv.at[3], low),
    ]
    for copy in halos:
        copy.start()

    boxes = [
        (p_out, p_in), (a_out, a_in), (s_out, s_in), (q_out, q_in), (b_out, b_in), (u_out, u_in)
    ]
    MAT_F, VEC_F, BACK_F, MAT_B, VEC_B, BACK_B = range(6)

    def outgoing(kind, to):
        out, into = boxes[kind]
        return remote(
            out.at[to], into.at[me], sends.at[kind, to], recvs.at[kind, me], {"stream": to}
        )

    def wait_from(kind, source):
        out, into = boxes[kind]

        @pl.when(source != me)
        def _():
            remote(
                out.at[source], into.at[source], sends.at[kind, source],
                recvs.at[kind, source], {"stream": source},
            ).wait_recv()

    def send_some(kind, first, end):
        def one(o, carry):
            outgoing(kind, lax.rem(me + o, streams)).start()
            return carry

        lax.fori_loop(first, end, one, 0)

    def keep_own(kind, count):
        out, into = boxes[kind]

        def one(e, carry):
            into[me, e] = out[me, e]
            return carry

        lax.fori_loop(0, count, one, 0)

    def pack(out, e, value):
        for c in range(chunks):
            for i in range(per_chunk):
                out[c * per_chunk + i, e] = value[
                    i * piece : (i + 1) * piece, c * CHUNK : (c + 1) * CHUNK
                ]

    def get(ref, index, count):
        return [ref[(k, *index)] for k in range(count)]

    def put(ref, index, values):
        for k, value in enumerate(values):
            ref[(k, *index)] = value

    def own_plane(p, carry):
        put(prim, (p + 1,), primitive(get(state, (p,), 5)))
        return carry

    lax.fori_loop(0, planes, own_plane, 0)
    loads[1].wait()

    def matrices_f(p, carry):
        jac = half_jacobian(get(prim, (p,), 7))
        for r in range(5):
            row = [diag[5 * r + k, p] for k in range(5)]
            for k, value in enumerate(row_times(row, jac, 1.0)):
                mats_f[5 * r + k, p] = value
        return carry

    def matrices_b(p, carry):
        jac = half_jacobian(get(prim, (p + 2,), 7))
        for r in range(5):
            row = [-diag[5 * r + k, p] for k in range(5)]
            for k, value in enumerate(row_times(row, jac, -1.0)):
                mats_b[5 * r + k, p] = value
        return carry

    def multiply(mats, order, out):
        for n, p in enumerate(order[1:]):
            final = n == len(order) - 2

            def column(j, carry):
                if n == 0:
                    vec = [mats[5 * k + j, order[0]] for k in range(5)]
                else:
                    vec = [prod[5 * k + j] for k in range(5)]
                for r, value in enumerate(mat_vec(lambda e: mats[e, p], vec)):
                    if final:
                        pack(out, 5 * r + j, value)
                    else:
                        prod[5 * r + j] = value
                return carry

            lax.fori_loop(0, 5, column, 0)

    lax.fori_loop(1, planes, matrices_f, 0)
    halos[0].wait_recv()
    halos[1].wait_recv()
    below = [jnp.where(me == 0, free_values[k], halo_stream[0, k]) for k in range(5)]
    put(prim, (0,), primitive(below))
    above = [
        jnp.where(me == last, state[k, planes - 1], halo_stream[1, k]) for k in range(5)
    ]
    put(prim, (planes + 1,), primitive(above))
    matrices_f(0, 0)

    @pl.when((me > 0) & (me < last))
    def _():
        multiply(mats_f, list(range(planes)), p_out)
        send_some(MAT_F, 1, streams)
        keep_own(MAT_F, 25)

    def inner_face(f, carry):
        put(flux_stream, (f,), roe_twice(get(prim, (f,), 7), get(prim, (f + 1,), 7), 0))
        return carry

    lax.fori_loop(0, planes + 1, inner_face, 0)

    def span_plane(p, carry):
        cell = get(prim, (p + 1,), 7)
        ahead = [pltpu.roll(field, lanes - 1, 1) for field in cell]
        face = roe_twice(cell, ahead, 2)
        put(res, (p,), [f - pltpu.roll(f, 1, 1) for f in face])
        return carry

    lax.fori_loop(0, planes, span_plane, 0)
    halos[2].wait_recv()
    halos[3].wait_recv()
    loads[2].wait()
    loads[3].wait()

    def ghost(cell, kinds):
        out = []
        for k in range(5):
            mirror = -cell[k] if k == 2 else cell[k]
            out.append(
                jnp.where(kinds == 0, mirror, jnp.where(kinds == 1, cell[k], free_values[k]))
            )
        return out

    row_first = [edge[0, k] for k in range(5)]
    row_last = [edge[1, k] for k in range(5)]
    ghost_low = ghost(row_first, kinds_low[...])
    ghost_high = ghost(row_last, kinds_high[...])
    side_low = [jnp.where(mine == 0, ghost_low[k], halo_cross[0, k]) for k in range(5)]
    side_high = [
        jnp.where(mine == crosses - 1, ghost_high[k], halo_cross[1, k]) for k in range(5)
    ]
    put(low_prim, (), primitive(side_low))
    put(top_flux, (), roe_twice(primitive(row_last), primitive(side_high), 1))

    row_no = lax.broadcasted_iota(jnp.int32, (rows, lanes), 0)

    def plane_residual(p, carry):
        cell = get(prim, (p + 1,), 7)
        under = [
            jnp.where(row_no == 0, low_prim[k, pl.ds(p, 1), :], pltpu.roll(cell[k], 1, 0))
            for k in range(7)
        ]
        face = roe_twice(under, cell, 1)
        for k in range(5):
            over = jnp.where(
                row_no == rows - 1,
                top_flux[k, pl.ds(p, 1), :],
                pltpu.roll(face[k], rows - 1, 0),
            )
            res[k, p] = 0.5 * (
                (flux_stream[k, p + 1] - flux_stream[k, p]) + (over - face[k]) + res[k, p]
            )
        return carry

    lax.fori_loop(0, planes, plane_residual, 0)
    save_res = pltpu.make_async_copy(res, res_hbm, save_sem.at[0])
    save_res.start()

    def plane_drive(p, previous):
        u, v, s, phi, enth, lam, u1, _, _ = half_jacobian(get(prim, (p,), 7))
        own = u + lam
        q = previous[1] - u1 * previous[0]
        pres = (
            phi * previous[0]
            - 0.4 * (u * previous[1] + v * previous[2] + s * previous[3])
            + 0.2 * previous[4]
        )
        term = [
            0.5 * previous[1] + lam * previous[0],
            own * previous[1] + u * q + pres,
            own * previous[2] + v * q,
            own * previous[3] + s * q,
            own * previous[4] + u1 * pres + enth * q,
        ]
        out = mat_vec(lambda e: diag[e, p], [term[k] - res[k, p] for k in range(5)])
        put(drive, (p,), out)
        return tuple(out)

    zero = jnp.zeros((rows, lanes), jnp.float32)
    ahead = lax.fori_loop(0, planes, plane_drive, (zero,) * 5)
    for k in range(5):
        pack(a_out, k, ahead[k])

    @pl.when(me < last)
    def _():
        send_some(VEC_F, 1, streams)
        keep_own(VEC_F, 5)

    lax.fori_loop(0, planes, matrices_b, 0)
    half = streams // 2

    @pl.when((me > 0) & (me < last))
    def _():
        multiply(mats_b, list(reversed(range(planes))), q_out)
        send_some(MAT_B, 1, half)
        keep_own(MAT_B, 25)

    def hand_back(kind, to, values):
        out, into = boxes[kind]
        for k in range(5):
            out[to, k] = values[k]

        @pl.when(to != me)
        def _():
            outgoing(kind, to).start()

        @pl.when(to == me)
        def _():
            for k in range(5):
                into[me, k] = values[k]

    wait_from(VEC_F, 0)
    current = [a_in[0, k] for k in range(5)]
    hand_back(BACK_F, 1, current)

    def scan_f(j, vec):
        wait_from(MAT_F, j)
        wait_from(VEC_F, j)
        step = mat_vec(lambda e: p_in[j, e], vec)
        out = [a_in[j, k] + step[k] for k in range(5)]
        hand_back(BACK_F, j + 1, out)
        return tuple(out)

    lax.fori_loop(1, last, scan_f, tuple(current))

    @pl.when((me > 0) & (me < last))
    def _():
        send_some(MAT_B, half, streams)

    def spot(c):
        return pl.ds(pl.multiple_of(c * CHUNK, CHUNK), CHUNK)

    def gather(kind, c):
        for i in range(per_chunk):
            wait_from(kind, c * per_chunk + i)

    def joined(into, c, k):
        parts = [into[c * per_chunk + i, k] for i in range(per_chunk)]
        return parts[0] if per_chunk == 1 else jnp.concatenate(parts, axis=0)

    def settle(c, carry):
        at = spot(c)

        @pl.when(me > 0)
        def _():
            gather(BACK_F, c)

        delta = [jnp.where(me == 0, 0.0, joined(s_in, c, k)) for k in range(5)]
        star = []
        for p in range(planes):
            delta = mat_vec(lambda e: mats_f[e, p, :, at], delta)
            star.append([drive[k, p, :, at] + delta[k] for k in range(5)])
        current = star[planes - 1]
        for p in reversed(range(planes)):
            if p < planes - 1:
                step = mat_vec(lambda e: mats_b[e, p, :, at], current)
                current = [star[p][k] + step[k] for k in range(5)]
            for k in range(5):
                base[k, p, :, at] = current[k]
        for i in range(per_chunk):
            to = c * per_chunk + i
            for k in range(5):
                b_out[to, k] = current[k][i * piece : (i + 1) * piece]

            @pl.when((me > 0) & (to != me))
            def _():
                outgoing(VEC_B, to).start()

        return carry

    lax.fori_loop(0, chunks, settle, 0)
    keep_own(VEC_B, 5)

    wait_from(VEC_B, last)
    current = [b_in[last, k] for k in range(5)]
    hand_back(BACK_B, last - 1, current)

    def scan_b(n, vec):
        j = last - n
        wait_from(MAT_B, j)
        wait_from(VEC_B, j)
        step = mat_vec(lambda e: q_in[j, e], vec)
        out = [b_in[j, k] + step[k] for k in range(5)]
        hand_back(BACK_B, j - 1, out)
        return tuple(out)

    lax.fori_loop(1, last, scan_b, tuple(current))

    def finish(c, carry):
        at = spot(c)

        @pl.when(me < last)
        def _():
            gather(BACK_B, c)

        delta = [jnp.where(me == last, 0.0, joined(u_in, c, k)) for k in range(5)]
        for p in reversed(range(planes)):
            delta = mat_vec(lambda e: mats_b[e, p, :, at], delta)
            for k in range(5):
                upd[k, p, :, at] = base[k, p, :, at] + delta[k]
        return carry

    lax.fori_loop(0, chunks, finish, 0)
    save_upd = pltpu.make_async_copy(upd, upd_hbm, save_sem.at[1])
    save_upd.start()

    for copy in halos:
        copy.wait_send()

    def sent(kind):
        def one(o, carry):
            outgoing(kind, lax.rem(me + o, streams)).wait_send()
            return carry

        lax.fori_loop(1, streams, one, 0)

    @pl.when((me > 0) & (me < last))
    def _():
        sent(MAT_F)
        sent(MAT_B)

    @pl.when(me < last)
    def _():
        sent(VEC_F)

    @pl.when(me > 0)
    def _():
        sent(VEC_B)

    def sent_back(t, carry):
        @pl.when(t != me)
        def _():
            outgoing(BACK_F, t).wait_send()

        @pl.when(t - 1 != me)
        def _():
            outgoing(BACK_B, t - 1).wait_send()

        return carry

    lax.fori_loop(1, streams, sent_back, 0)
    save_res.wait()
    save_upd.wait()


def local(streams, crosses, state, diag, kinds_low, kinds_high):
    _, planes, rows, lanes = state.shape
    piece = rows * (lanes // CHUNK) // streams
    f32 = jnp.float32
    block = (planes, rows, lanes)

    def vmem(*shape):
        return pltpu.VMEM(shape, f32)

    return pl.pallas_call(
        functools.partial(kernel, streams, crosses),
        out_shape=[jax.ShapeDtypeStruct(state.shape, f32)] * 2,
        in_specs=[pl.BlockSpec(memory_space=pl.ANY)] * 4,
        out_specs=[pl.BlockSpec(memory_space=pl.ANY)] * 2,
        scratch_shapes=[
            vmem(5, *block),
            vmem(25, *block),
            pltpu.VMEM((planes, lanes), jnp.int32),
            pltpu.VMEM((planes, lanes), jnp.int32),
            vmem(7, planes + 2, rows, lanes),
            vmem(2, 5, planes, lanes),
            vmem(2, 5, planes, lanes),
            vmem(2, 5, rows, lanes),
            vmem(7, planes, lanes),
            vmem(5, planes, lanes),
            vmem(5, planes + 1, rows, lanes),
            vmem(5, *block),
            vmem(5, *block),
            vmem(25, *block),
            vmem(25, *block),
            vmem(25, rows, lanes),
            vmem(5, *block),
            vmem(5, *block),
            *[vmem(streams, 25, piece, CHUNK)] * 4,
            *[vmem(streams, 5, piece, CHUNK)] * 8,
            pltpu.SemaphoreType.DMA((4,)),
            pltpu.SemaphoreType.DMA((2,)),
            pltpu.SemaphoreType.DMA((4,)),
            pltpu.SemaphoreType.DMA((4,)),
            pltpu.SemaphoreType.DMA((6, streams)),
            pltpu.SemaphoreType.DMA((6, streams)),
        ],
        compiler_params=pltpu.CompilerParams(
            collective_id=0, has_side_effects=True, vmem_limit_bytes=60 * 2**20
        ),
        cost_estimate=pl.CostEstimate(
            flops=16000000, bytes_accessed=2700000, transcendentals=100000
        ),
    )(state, diag, kinds_low, kinds_high)


def solution(mesh):
    spec = P(None, "stream", "cross", None)
    return jax.shard_map(
        functools.partial(local, mesh.shape["stream"], mesh.shape["cross"]),
        mesh=mesh,
        in_specs=(spec, spec, P("stream", None), P("stream", None)),
        out_specs=(spec, spec),
        check_vma=False,
    )
```

```python
import functools

import jax
import jax.numpy as jnp
from jax import lax
from jax.experimental import pallas as pl
from jax.experimental.pallas import tpu as pltpu
from jax.sharding import PartitionSpec as P

MESH = pl.DeviceIdType.MESH
free_values = (1.0, 0.0, 0.0, 0.0, 2.5)
CHUNK = 128
RHO, U1, U2, U3, PRES, ENTH, ROOT = range(7)


def primitive(q):
    inv_root = lax.rsqrt(q[0])
    inv = inv_root * inv_root
    u = [q[1] * inv, q[2] * inv, q[3] * inv]
    pressure = 0.4 * (q[4] - 0.5 * (q[1] * u[0] + q[2] * u[1] + q[3] * u[2]))
    return [q[0], *u, pressure, (q[4] + pressure) * inv, q[0] * inv_root]


def roe_twice(left, right, d):
    share = right[ROOT] / (left[ROOT] + right[ROOT])
    jump = [right[1 + k] - left[1 + k] for k in range(3)]
    avg = [left[1 + k] + share * jump[k] for k in range(3)]
    enth = left[ENTH] + share * (right[ENTH] - left[ENTH])
    kinetic = 0.5 * (avg[0] * avg[0] + avg[1] * avg[1] + avg[2] * avg[2])
    sound_sq = 0.4 * (enth - kinetic)
    inv_sound = lax.rsqrt(sound_sq)
    sound = sound_sq * inv_sound
    inv_sq = inv_sound * inv_sound
    dens = left[ROOT] * right[ROOT]
    normal = avg[d]
    scaled_pres = (right[PRES] - left[PRES]) * inv_sq
    scaled_jump = dens * inv_sound * jump[d]
    slow = jnp.abs(normal - sound) * (0.5 * (scaled_pres - scaled_jump))
    fast = jnp.abs(normal + sound) * (0.5 * (scaled_pres + scaled_jump))
    speed = jnp.abs(normal)
    entropy = speed * (right[RHO] - left[RHO] - scaled_pres)
    shear = speed * dens
    acoustic = slow + fast
    total = acoustic + entropy
    spread = (fast - slow) * sound
    mass_left = left[RHO] * left[1 + d]
    mass_right = right[RHO] * right[1 + d]
    pieces = [mass_left + mass_right - total]
    along = 0.0
    for k in range(3):
        central = mass_left * left[1 + k] + mass_right * right[1 + k]
        if k == d:
            pieces.append(central + (left[PRES] + right[PRES]) - (total * avg[k] + spread))
        else:
            pieces.append(central - (total * avg[k] + shear * jump[k]))
            along = along + avg[k] * jump[k]
    pieces.append(
        mass_left * left[ENTH]
        + mass_right * right[ENTH]
        - (acoustic * enth + spread * normal + entropy * kinetic + shear * along)
    )
    return pieces


def half_jacobian(w):
    u, v, s = 0.5 * w[U1], 0.5 * w[U2], 0.5 * w[U3]
    phi = 0.1 * (w[U1] * w[U1] + w[U2] * w[U2] + w[U3] * w[U3])
    inv_root = w[ROOT] / w[RHO]
    pos = 1.4 * w[PRES]
    lam = jnp.abs(u) + 0.5 * (pos * lax.rsqrt(pos) * inv_root)
    return u, v, s, phi, 0.5 * w[ENTH], lam, w[U1], w[U2], w[U3]


def row_times(row, jac, sign):
    u, v, s, phi, enth, lam, u1, _, _ = jac
    pres = row[1] + u1 * row[4]
    move = u * row[1] + v * row[2] + s * row[3] + enth * row[4]
    own = u + sign * lam
    return [
        phi * pres - u1 * move + (sign * lam) * row[0],
        0.5 * row[0] + own * row[1] + move - 0.4 * (u * pres),
        own * row[2] - 0.4 * (v * pres),
        own * row[3] - 0.4 * (s * pres),
        own * row[4] + 0.2 * pres,
    ]


def half_apply(jac, vec, sign):
    u, v, s, phi, enth, lam, u1, _, _ = jac
    own = u + sign * lam
    q = vec[1] - u1 * vec[0]
    pres = phi * vec[0] - 0.4 * (u * vec[1] + v * vec[2] + s * vec[3]) + 0.2 * vec[4]
    return [
        0.5 * vec[1] + (sign * lam) * vec[0],
        own * vec[1] + u * q + pres,
        own * vec[2] + v * q,
        own * vec[3] + s * q,
        own * vec[4] + u1 * pres + enth * q,
    ]


def mat_vec(load, vec):
    out = []
    for r in range(5):
        term = [load(5 * r + k) * vec[k] for k in range(5)]
        out.append((term[0] + term[1]) + (term[2] + term[3]) + term[4])
    return out


def kernel(
    streams, crosses,
    state_hbm, diag_hbm, kinds_hbm, res, upd,
    state, diag, kinds, prim, edge, halo_cross, halo_stream, low_prim, top_flux,
    flux_stream, drive, mats_f, mats_b, base,
    p_out, p_in, q_out, q_in, a_out, a_in, s_out, s_in, b_out, b_in, u_out, u_in,
    load_sem, halo_send, halo_recv, sends, recvs,
):
    me = lax.axis_index("stream")
    mine = lax.axis_index("cross")
    planes, rows, lanes = state.shape[1:]
    chunks = lanes // CHUNK
    piece = rows * chunks // streams
    per_chunk = rows // piece
    last = streams - 1
    up = {"stream": lax.rem(me + 1, streams)}
    down = {"stream": lax.rem(me + last, streams)}
    high = {"cross": lax.rem(mine + 1, crosses)}
    low = {"cross": lax.rem(mine + crosses - 1, crosses)}

    loads = [
        pltpu.make_async_copy(src, dst, load_sem.at[i])
        for i, (src, dst) in enumerate(
            [(state_hbm, state), (diag_hbm, diag), (kinds_hbm, kinds)]
        )
    ]
    for copy in loads:
        copy.start()
    barrier = pltpu.get_barrier_semaphore()

    def greet(o, carry):
        pl.semaphore_signal(
            barrier, inc=1, device_id={"stream": lax.rem(me + o, streams)}, device_id_type=MESH
        )
        return carry

    lax.fori_loop(1, streams, greet, 0)
    for to in (high, low):
        pl.semaphore_signal(barrier, inc=1, device_id=to, device_id_type=MESH)

    def get(ref, index, count):
        return [ref[(k, *index)] for k in range(count)]

    def put(ref, index, values):
        for k, value in enumerate(values):
            ref[(k, *index)] = value

    def pack(out, e, value):
        for c in range(chunks):
            for i in range(per_chunk):
                out[c * per_chunk + i, e] = value[
                    i * piece : (i + 1) * piece, c * CHUNK : (c + 1) * CHUNK
                ]

    def matrices_f(p, carry):
        jac = half_jacobian(get(prim, (p,), 7))
        for r in range(5):
            row = [diag[5 * r + k, p] for k in range(5)]
            for k, value in enumerate(row_times(row, jac, 1.0)):
                mats_f[5 * r + k, p] = value
        return carry

    def matrices_b(p, carry):
        jac = half_jacobian(get(prim, (p + 2,), 7))
        for r in range(5):
            row = [-diag[5 * r + k, p] for k in range(5)]
            for k, value in enumerate(row_times(row, jac, -1.0)):
                mats_b[5 * r + k, p] = value
        return carry

    def product_f(j, carry):
        vec = [diag[5 * k + j, 0] for k in range(5)]
        for p in range(1, planes):
            vec = mat_vec(lambda e: mats_f[e, p], vec)
        vec = half_apply(half_jacobian(get(prim, (planes,), 7)), vec, 1.0)
        for r in range(5):
            pack(p_out, 5 * r + j, vec[r])
        return carry

    def product_b(j, carry):
        vec = [-diag[5 * k + j, planes - 1] for k in range(5)]
        for p in reversed(range(planes - 1)):
            vec = mat_vec(lambda e: mats_b[e, p], vec)
        vec = half_apply(half_jacobian(get(prim, (1,), 7)), vec, -1.0)
        for r in range(5):
            pack(q_out, 5 * r + j, vec[r])
        return carry

    def own_plane(p, carry):
        put(prim, (p + 1,), primitive(get(state, (p,), 5)))
        return carry

    loads[0].wait()
    for p in range(planes):
        for k in range(5):
            edge[0, k, pl.ds(p, 1), :] = state[k, p, pl.ds(0, 1), :]
            edge[1, k, pl.ds(p, 1), :] = state[k, p, pl.ds(rows - 1, 1), :]
    lax.fori_loop(0, planes, own_plane, 0)
    loads[1].wait()
    lax.fori_loop(1, planes, matrices_f, 0)
    lax.fori_loop(0, 5, product_f, 0)
    pl.semaphore_wait(barrier, streams + 1)

    def remote(src, dst, send, recv, to):
        return pltpu.make_async_remote_copy(
            src_ref=src, dst_ref=dst, send_sem=send, recv_sem=recv,
            device_id=to, device_id_type=MESH,
        )

    halos = [
        remote(state.at[:, planes - 1], halo_stream.at[0], halo_send.at[0], halo_recv.at[0], up),
        remote(state.at[:, 0], halo_stream.at[1], halo_send.at[1], halo_recv.at[1], down),
        remote(edge.at[1], halo_cross.at[0], halo_send.at[2], halo_recv.at[2], high),
        remote(edge.at[0], halo_cross.at[1], halo_send.at[3], halo_recv.at[3], low),
    ]
    for copy in halos:
        copy.start()

    boxes = [
        (p_out, p_in), (a_out, a_in), (s_out, s_in), (q_out, q_in), (b_out, b_in), (u_out, u_in)
    ]
    MAT_F, VEC_F, BACK_F, MAT_B, VEC_B, BACK_B = range(6)

    def outgoing(kind, to):
        out, into = boxes[kind]
        return remote(
            out.at[to], into.at[me], sends.at[kind, to], recvs.at[kind, me], {"stream": to}
        )

    def wait_from(kind, source):
        out, into = boxes[kind]

        @pl.when(source != me)
        def _():
            remote(
                out.at[source], into.at[source], sends.at[kind, source],
                recvs.at[kind, source], {"stream": source},
            ).wait_recv()

    def send_some(kind, first, end):
        def one(o, carry):
            outgoing(kind, lax.rem(me + o, streams)).start()
            return carry

        lax.fori_loop(first, end, one, 0)

    def sent(kind):
        def one(o, carry):
            outgoing(kind, lax.rem(me + o, streams)).wait_send()
            return carry

        lax.fori_loop(1, streams, one, 0)

    def keep_own(kind, count):
        out, into = boxes[kind]

        def one(e, carry):
            into[me, e] = out[me, e]
            return carry

        lax.fori_loop(0, count, one, 0)

    inner = (me > 0) & (me < last)

    @pl.when(inner)
    def _():
        send_some(MAT_F, 1, streams)

    def inner_face(f, carry):
        put(flux_stream, (f,), roe_twice(get(prim, (f,), 7), get(prim, (f + 1,), 7), 0))
        return carry

    def span_plane(p, carry):
        cell = get(prim, (p + 1,), 7)
        ahead = [pltpu.roll(field, lanes - 1, 1) for field in cell]
        face = roe_twice(cell, ahead, 2)
        put(res, (p,), [f - pltpu.roll(f, 1, 1) for f in face])
        return carry

    lax.fori_loop(0, planes, span_plane, 0)
    lax.fori_loop(1, planes, inner_face, 0)
    halos[0].wait_recv()
    halos[1].wait_recv()
    below = [jnp.where(me == 0, free_values[k], halo_stream[0, k]) for k in range(5)]
    put(prim, (0,), primitive(below))
    above = [
        jnp.where(me == last, state[k, planes - 1], halo_stream[1, k]) for k in range(5)
    ]
    put(prim, (planes + 1,), primitive(above))
    lax.fori_loop(0, 2, lambda i, c: inner_face(i * planes, c), 0)
    halos[2].wait_recv()
    halos[3].wait_recv()
    loads[2].wait()

    def ghost(cell, kinds):
        out = []
        for k in range(5):
            mirror = -cell[k] if k == 2 else cell[k]
            out.append(
                jnp.where(kinds == 0, mirror, jnp.where(kinds == 1, cell[k], free_values[k]))
            )
        return out

    row_first = [edge[0, k] for k in range(5)]
    row_last = [edge[1, k] for k in range(5)]
    ghost_low = ghost(row_first, kinds[...] & 3)
    ghost_high = ghost(row_last, kinds[...] >> 2)
    side_low = [jnp.where(mine == 0, ghost_low[k], halo_cross[0, k]) for k in range(5)]
    side_high = [
        jnp.where(mine == crosses - 1, ghost_high[k], halo_cross[1, k]) for k in range(5)
    ]
    put(low_prim, (), primitive(side_low))
    put(top_flux, (), roe_twice(primitive(row_last), primitive(side_high), 1))

    row_no = lax.broadcasted_iota(jnp.int32, (rows, lanes), 0)

    def plane_residual(p, carry):
        cell = get(prim, (p + 1,), 7)
        under = [
            jnp.where(row_no == 0, low_prim[k, pl.ds(p, 1), :], pltpu.roll(cell[k], 1, 0))
            for k in range(7)
        ]
        face = roe_twice(under, cell, 1)
        for k in range(5):
            over = jnp.where(
                row_no == rows - 1,
                top_flux[k, pl.ds(p, 1), :],
                pltpu.roll(face[k], rows - 1, 0),
            )
            res[k, p] = 0.5 * (
                (flux_stream[k, p + 1] - flux_stream[k, p]) + (over - face[k]) + res[k, p]
            )
        return carry

    lax.fori_loop(0, planes, plane_residual, 0)
    def plane_drive(p, previous):
        term = half_apply(half_jacobian(get(prim, (p,), 7)), previous, 1.0)
        out = mat_vec(lambda e: diag[e, p], [term[k] - res[k, p] for k in range(5)])
        put(drive, (p,), out)
        return tuple(out)

    current = mat_vec(lambda e: diag[e, 0], [-res[k, 0] for k in range(5)])
    put(drive, (0,), current)
    current = lax.fori_loop(1, planes, plane_drive, tuple(current))
    current = half_apply(half_jacobian(get(prim, (planes,), 7)), current, 1.0)
    for k in range(5):
        pack(a_out, k, current[k])

    @pl.when(me < last)
    def _():
        send_some(VEC_F, 1, streams)

    keep_own(MAT_F, 25)
    keep_own(VEC_F, 5)
    lax.fori_loop(0, planes - 1, matrices_b, 0)
    lax.fori_loop(0, 5, product_b, 0)
    keep_own(MAT_B, 25)
    half = streams // 2

    @pl.when(inner)
    def _():
        sent(MAT_F)
        send_some(MAT_B, 1, half)

    def hand_back(kind, to, values):
        out, into = boxes[kind]
        for k in range(5):
            out[to, k] = values[k]

        @pl.when(to != me)
        def _():
            outgoing(kind, to).start()

        @pl.when(to == me)
        def _():
            for k in range(5):
                into[me, k] = values[k]

    wait_from(VEC_F, 0)
    current = [a_in[0, k] for k in range(5)]
    hand_back(BACK_F, 1, current)

    def scan_f(j, vec):
        wait_from(MAT_F, j)
        wait_from(VEC_F, j)
        step = mat_vec(lambda e: p_in[j, e], vec)
        out = [a_in[j, k] + step[k] for k in range(5)]
        hand_back(BACK_F, j + 1, out)
        return tuple(out)

    lax.fori_loop(1, last, scan_f, tuple(current))

    @pl.when(inner)
    def _():
        send_some(MAT_B, half, streams)

    def gather(kind):
        def one(j, carry):
            wait_from(kind, j)
            return carry

        lax.fori_loop(0, streams, one, 0)

    def joined(into, k):
        wide = []
        for c in range(chunks):
            parts = [into[c * per_chunk + i, k] for i in range(per_chunk)]
            wide.append(parts[0] if per_chunk == 1 else jnp.concatenate(parts, axis=0))
        return wide[0] if chunks == 1 else jnp.concatenate(wide, axis=1)

    @pl.when(me > 0)
    def _():
        gather(BACK_F)

    delta = [jnp.where(me == 0, 0.0, joined(s_in, k)) for k in range(5)]
    for p in range(planes):
        delta = mat_vec(lambda e: diag[e, 0] if p == 0 else mats_f[e, p], delta)
        current = [drive[k, p] + delta[k] for k in range(5)]
        put(base, (p,), current)
    for p in reversed(range(planes - 1)):
        step = mat_vec(lambda e: mats_b[e, p], current)
        current = [base[k, p] + step[k] for k in range(5)]
        put(base, (p,), current)
    current = half_apply(half_jacobian(get(prim, (1,), 7)), current, -1.0)
    for k in range(5):
        pack(b_out, k, current[k])

    @pl.when(me > 0)
    def _():
        send_some(VEC_B, 1, streams)

    keep_own(VEC_B, 5)

    wait_from(VEC_B, last)
    current = [b_in[last, k] for k in range(5)]
    hand_back(BACK_B, last - 1, current)

    def scan_b(n, vec):
        j = last - n
        wait_from(MAT_B, j)
        wait_from(VEC_B, j)
        step = mat_vec(lambda e: q_in[j, e], vec)
        out = [b_in[j, k] + step[k] for k in range(5)]
        hand_back(BACK_B, j - 1, out)
        return tuple(out)

    lax.fori_loop(1, last, scan_b, tuple(current))

    @pl.when(me < last)
    def _():
        gather(BACK_B)

    delta = [jnp.where(me == last, 0.0, joined(u_in, k)) for k in range(5)]
    for p in reversed(range(planes)):
        if p == planes - 1:
            delta = [-d for d in mat_vec(lambda e: diag[e, p], delta)]
        else:
            delta = mat_vec(lambda e: mats_b[e, p], delta)
        for k in range(5):
            upd[k, p] = base[k, p] + delta[k]

    for copy in halos:
        copy.wait_send()

    @pl.when(inner)
    def _():
        sent(MAT_B)

    @pl.when(me < last)
    def _():
        sent(VEC_F)

    @pl.when(me > 0)
    def _():
        sent(VEC_B)

    def sent_back(t, carry):
        @pl.when(t != me)
        def _():
            outgoing(BACK_F, t).wait_send()

        @pl.when(t - 1 != me)
        def _():
            outgoing(BACK_B, t - 1).wait_send()

        return carry

    lax.fori_loop(1, streams, sent_back, 0)


def local(streams, crosses, state, diag, kinds_low, kinds_high):
    _, planes, rows, lanes = state.shape
    piece = rows * (lanes // CHUNK) // streams
    f32 = jnp.float32
    block = (planes, rows, lanes)

    def vmem(*shape):
        return pltpu.VMEM(shape, f32)

    return pl.pallas_call(
        functools.partial(kernel, streams, crosses),
        out_shape=[jax.ShapeDtypeStruct(state.shape, f32)] * 2,
        in_specs=[pl.BlockSpec(memory_space=pltpu.HBM)] * 3,
        out_specs=[pl.BlockSpec(memory_space=pltpu.VMEM)] * 2,
        scratch_shapes=[
            vmem(5, *block),
            vmem(25, *block),
            pltpu.VMEM((planes, lanes), jnp.int32),
            vmem(7, planes + 2, rows, lanes),
            vmem(2, 5, planes, lanes),
            vmem(2, 5, planes, lanes),
            vmem(2, 5, rows, lanes),
            vmem(7, planes, lanes),
            vmem(5, planes, lanes),
            vmem(5, planes + 1, rows, lanes),
            vmem(5, *block),
            vmem(25, *block),
            vmem(25, *block),
            vmem(5, *block),
            *[vmem(streams, 25, piece, CHUNK)] * 4,
            *[vmem(streams, 5, piece, CHUNK)] * 8,
            pltpu.SemaphoreType.DMA((3,)),
            pltpu.SemaphoreType.DMA((4,)),
            pltpu.SemaphoreType.DMA((4,)),
            pltpu.SemaphoreType.DMA((6, streams)),
            pltpu.SemaphoreType.DMA((6, streams)),
        ],
        compiler_params=pltpu.CompilerParams(
            collective_id=0, has_side_effects=True, vmem_limit_bytes=54400 * 1024
        ),
        cost_estimate=pl.CostEstimate(
            flops=16000000, bytes_accessed=2700000, transcendentals=100000
        ),
    )(state, diag, kinds_low + 4 * kinds_high)


def solution(mesh):
    spec = P(None, "stream", "cross", None)
    return jax.shard_map(
        functools.partial(local, mesh.shape["stream"], mesh.shape["cross"]),
        mesh=mesh,
        in_specs=(spec, spec, P("stream", None), P("stream", None)),
        out_specs=(spec, spec),
        check_vma=False,
    )
```

```python
import functools

import jax
import jax.numpy as jnp
from jax import lax
from jax.experimental import pallas as pl
from jax.experimental.pallas import tpu as pltpu
from jax.sharding import PartitionSpec as P

MESH = pl.DeviceIdType.MESH
free_values = (1.0, 0.0, 0.0, 0.0, 2.5)
CHUNK = 128
RHO, U1, U2, U3, PRES, ENTH, ROOT = range(7)


def primitive(q):
    inv_root = lax.rsqrt(q[0])
    inv = inv_root * inv_root
    u = [q[1] * inv, q[2] * inv, q[3] * inv]
    pressure = 0.4 * (q[4] - 0.5 * (q[1] * u[0] + q[2] * u[1] + q[3] * u[2]))
    return [q[0], *u, pressure, (q[4] + pressure) * inv, q[0] * inv_root]


def roe_twice(left, right, d):
    share = right[ROOT] / (left[ROOT] + right[ROOT])
    jump = [right[1 + k] - left[1 + k] for k in range(3)]
    avg = [left[1 + k] + share * jump[k] for k in range(3)]
    enth = left[ENTH] + share * (right[ENTH] - left[ENTH])
    kinetic = 0.5 * (avg[0] * avg[0] + avg[1] * avg[1] + avg[2] * avg[2])
    sound_sq = 0.4 * (enth - kinetic)
    inv_sound = lax.rsqrt(sound_sq)
    sound = sound_sq * inv_sound
    inv_sq = inv_sound * inv_sound
    dens = left[ROOT] * right[ROOT]
    normal = avg[d]
    scaled_pres = (right[PRES] - left[PRES]) * inv_sq
    scaled_jump = dens * inv_sound * jump[d]
    slow = jnp.abs(normal - sound) * (0.5 * (scaled_pres - scaled_jump))
    fast = jnp.abs(normal + sound) * (0.5 * (scaled_pres + scaled_jump))
    speed = jnp.abs(normal)
    entropy = speed * (right[RHO] - left[RHO] - scaled_pres)
    shear = speed * dens
    acoustic = slow + fast
    total = acoustic + entropy
    spread = (fast - slow) * sound
    mass_left = left[RHO] * left[1 + d]
    mass_right = right[RHO] * right[1 + d]
    pieces = [mass_left + mass_right - total]
    along = 0.0
    for k in range(3):
        central = mass_left * left[1 + k] + mass_right * right[1 + k]
        if k == d:
            pieces.append(central + (left[PRES] + right[PRES]) - (total * avg[k] + spread))
        else:
            pieces.append(central - (total * avg[k] + shear * jump[k]))
            along = along + avg[k] * jump[k]
    pieces.append(
        mass_left * left[ENTH]
        + mass_right * right[ENTH]
        - (acoustic * enth + spread * normal + entropy * kinetic + shear * along)
    )
    return pieces


def half_jacobian(w):
    u, v, s = 0.5 * w[U1], 0.5 * w[U2], 0.5 * w[U3]
    phi = 0.1 * (w[U1] * w[U1] + w[U2] * w[U2] + w[U3] * w[U3])
    inv_root = w[ROOT] / w[RHO]
    pos = 1.4 * w[PRES]
    lam = jnp.abs(u) + 0.5 * (pos * lax.rsqrt(pos) * inv_root)
    return u, v, s, phi, 0.5 * w[ENTH], lam, w[U1], w[U2], w[U3]


def row_times(row, jac, sign):
    u, v, s, phi, enth, lam, u1, _, _ = jac
    pres = row[1] + u1 * row[4]
    move = u * row[1] + v * row[2] + s * row[3] + enth * row[4]
    own = u + sign * lam
    return [
        phi * pres - u1 * move + (sign * lam) * row[0],
        0.5 * row[0] + own * row[1] + move - 0.4 * (u * pres),
        own * row[2] - 0.4 * (v * pres),
        own * row[3] - 0.4 * (s * pres),
        own * row[4] + 0.2 * pres,
    ]


def half_apply(jac, vec, sign):
    u, v, s, phi, enth, lam, u1, _, _ = jac
    own = u + sign * lam
    q = vec[1] - u1 * vec[0]
    pres = phi * vec[0] - 0.4 * (u * vec[1] + v * vec[2] + s * vec[3]) + 0.2 * vec[4]
    return [
        0.5 * vec[1] + (sign * lam) * vec[0],
        own * vec[1] + u * q + pres,
        own * vec[2] + v * q,
        own * vec[3] + s * q,
        own * vec[4] + u1 * pres + enth * q,
    ]


def mat_vec(load, vec):
    out = []
    for r in range(5):
        term = [load(5 * r + k) * vec[k] for k in range(5)]
        out.append((term[0] + term[1]) + (term[2] + term[3]) + term[4])
    return out


def kernel(
    streams, crosses,
    state_hbm, diag_hbm, kinds_hbm, res, upd,
    state, diag, kinds, prim, edge, halo_cross, halo_stream, low_prim, top_flux,
    flux_stream, drive, mats_f, mats_b, base,
    p_out, p_in, q_out, q_in, a_out, a_in, s_out, s_in, b_out, b_in, u_out, u_in,
    load_sem, halo_send, halo_recv, sends, recvs,
):
    me = lax.axis_index("stream")
    mine = lax.axis_index("cross")
    planes, rows, lanes = state.shape[1:]
    chunks = lanes // CHUNK
    piece = rows * chunks // streams
    per_chunk = rows // piece
    last = streams - 1
    up = {"stream": lax.rem(me + 1, streams)}
    down = {"stream": lax.rem(me + last, streams)}
    high = {"cross": lax.rem(mine + 1, crosses)}
    low = {"cross": lax.rem(mine + crosses - 1, crosses)}

    loads = [
        pltpu.make_async_copy(src, dst, load_sem.at[i])
        for i, (src, dst) in enumerate(
            [(state_hbm, state), (diag_hbm, diag), (kinds_hbm, kinds)]
        )
    ]
    for copy in loads:
        copy.start()
    barrier = pltpu.get_barrier_semaphore()

    def greet(o, carry):
        pl.semaphore_signal(
            barrier, inc=1, device_id={"stream": lax.rem(me + o, streams)}, device_id_type=MESH
        )
        return carry

    lax.fori_loop(1, streams, greet, 0)
    for to in (high, low):
        pl.semaphore_signal(barrier, inc=1, device_id=to, device_id_type=MESH)

    def get(ref, index, count):
        return [ref[(k, *index)] for k in range(count)]

    def put(ref, index, values):
        for k, value in enumerate(values):
            ref[(k, *index)] = value

    def pack(out, e, value):
        for c in range(chunks):
            for i in range(per_chunk):
                out[c * per_chunk + i, e] = value[
                    i * piece : (i + 1) * piece, c * CHUNK : (c + 1) * CHUNK
                ]

    def matrices_f(p, carry):
        jac = half_jacobian(get(prim, (p,), 7))
        for r in range(5):
            row = [diag[5 * r + k, p] for k in range(5)]
            for k, value in enumerate(row_times(row, jac, 1.0)):
                mats_f[5 * r + k, p] = value
        return carry

    def matrices_b(p, carry):
        jac = half_jacobian(get(prim, (p + 2,), 7))
        for r in range(5):
            row = [-diag[5 * r + k, p] for k in range(5)]
            for k, value in enumerate(row_times(row, jac, -1.0)):
                mats_b[5 * r + k, p] = value
        return carry

    def product_f(j, carry):
        vec = [diag[5 * k + j, 0] for k in range(5)]
        for p in range(1, planes):
            vec = mat_vec(lambda e: mats_f[e, p], vec)
        vec = half_apply(half_jacobian(get(prim, (planes,), 7)), vec, 1.0)
        for r in range(5):
            pack(p_out, 5 * r + j, vec[r])
        return carry

    def product_b(j, carry):
        vec = [-diag[5 * k + j, planes - 1] for k in range(5)]
        for p in reversed(range(planes - 1)):
            vec = mat_vec(lambda e: mats_b[e, p], vec)
        vec = half_apply(half_jacobian(get(prim, (1,), 7)), vec, -1.0)
        for r in range(5):
            pack(q_out, 5 * r + j, vec[r])
        return carry

    def own_plane(p, carry):
        put(prim, (p + 1,), primitive(get(state, (p,), 5)))
        return carry

    loads[0].wait()
    for p in range(planes):
        for k in range(5):
            edge[0, k, pl.ds(p, 1), :] = state[k, p, pl.ds(0, 1), :]
            edge[1, k, pl.ds(p, 1), :] = state[k, p, pl.ds(rows - 1, 1), :]
    lax.fori_loop(0, planes, own_plane, 0)
    loads[1].wait()
    lax.fori_loop(1, planes, matrices_f, 0)
    lax.fori_loop(0, 5, product_f, 0)
    pl.semaphore_wait(barrier, streams + 1)

    def remote(src, dst, send, recv, to):
        return pltpu.make_async_remote_copy(
            src_ref=src, dst_ref=dst, send_sem=send, recv_sem=recv,
            device_id=to, device_id_type=MESH,
        )

    halos = [
        remote(state.at[:, planes - 1], halo_stream.at[0], halo_send.at[0], halo_recv.at[0], up),
        remote(state.at[:, 0], halo_stream.at[1], halo_send.at[1], halo_recv.at[1], down),
        remote(edge.at[1], halo_cross.at[0], halo_send.at[2], halo_recv.at[2], high),
        remote(edge.at[0], halo_cross.at[1], halo_send.at[3], halo_recv.at[3], low),
    ]
    for copy in halos:
        copy.start()

    boxes = [
        (p_out, p_in), (a_out, a_in), (s_out, s_in), (q_out, q_in), (b_out, b_in), (u_out, u_in)
    ]
    MAT_F, VEC_F, BACK_F, MAT_B, VEC_B, BACK_B = range(6)

    def outgoing(kind, to):
        out, into = boxes[kind]
        return remote(
            out.at[to], into.at[me], sends.at[kind, to], recvs.at[kind, me], {"stream": to}
        )

    def wait_from(kind, source):
        out, into = boxes[kind]

        @pl.when(source != me)
        def _():
            remote(
                out.at[source], into.at[source], sends.at[kind, source],
                recvs.at[kind, source], {"stream": source},
            ).wait_recv()

    def send_some(kind, first, end):
        def one(o, carry):
            outgoing(kind, lax.rem(me + o, streams)).start()
            return carry

        lax.fori_loop(first, end, one, 0)

    def sent(kind):
        def one(o, carry):
            outgoing(kind, lax.rem(me + o, streams)).wait_send()
            return carry

        lax.fori_loop(1, streams, one, 0)

    def keep_own(kind):
        out, into = boxes[kind]
        into[me] = out[me]

    def gather(kind, first, end):
        def one(j, carry):
            wait_from(kind, j)
            return carry

        lax.fori_loop(first, end, one, 0)

    def hand_back(kind, skip):
        def one(o, carry):
            to = lax.rem(me + o, streams)

            @pl.when(to != skip)
            def _():
                outgoing(kind, to).start()

            return carry

        lax.fori_loop(1, streams, one, 0)
        keep_own(kind)

    inner = (me > 0) & (me < last)

    @pl.when(inner)
    def _():
        send_some(MAT_F, 1, streams)

    def inner_face(f, carry):
        put(flux_stream, (f,), roe_twice(get(prim, (f,), 7), get(prim, (f + 1,), 7), 0))
        return carry

    def span_plane(p, carry):
        cell = get(prim, (p + 1,), 7)
        ahead = [pltpu.roll(field, lanes - 1, 1) for field in cell]
        face = roe_twice(cell, ahead, 2)
        put(res, (p,), [f - pltpu.roll(f, 1, 1) for f in face])
        return carry

    lax.fori_loop(0, planes, span_plane, 0)
    lax.fori_loop(1, planes, inner_face, 0)
    halos[0].wait_recv()
    halos[1].wait_recv()
    below = [jnp.where(me == 0, free_values[k], halo_stream[0, k]) for k in range(5)]
    put(prim, (0,), primitive(below))
    above = [
        jnp.where(me == last, state[k, planes - 1], halo_stream[1, k]) for k in range(5)
    ]
    put(prim, (planes + 1,), primitive(above))
    lax.fori_loop(0, 2, lambda i, c: inner_face(i * planes, c), 0)
    halos[2].wait_recv()
    halos[3].wait_recv()
    loads[2].wait()

    def ghost(cell, kinds):
        out = []
        for k in range(5):
            mirror = -cell[k] if k == 2 else cell[k]
            out.append(
                jnp.where(kinds == 0, mirror, jnp.where(kinds == 1, cell[k], free_values[k]))
            )
        return out

    row_first = [edge[0, k] for k in range(5)]
    row_last = [edge[1, k] for k in range(5)]
    ghost_low = ghost(row_first, kinds[...] & 3)
    ghost_high = ghost(row_last, kinds[...] >> 2)
    side_low = [jnp.where(mine == 0, ghost_low[k], halo_cross[0, k]) for k in range(5)]
    side_high = [
        jnp.where(mine == crosses - 1, ghost_high[k], halo_cross[1, k]) for k in range(5)
    ]
    put(low_prim, (), primitive(side_low))
    put(top_flux, (), roe_twice(primitive(row_last), primitive(side_high), 1))

    row_no = lax.broadcasted_iota(jnp.int32, (rows, lanes), 0)

    def plane_residual(p, carry):
        cell = get(prim, (p + 1,), 7)
        under = [
            jnp.where(row_no == 0, low_prim[k, pl.ds(p, 1), :], pltpu.roll(cell[k], 1, 0))
            for k in range(7)
        ]
        face = roe_twice(under, cell, 1)
        for k in range(5):
            over = jnp.where(
                row_no == rows - 1,
                top_flux[k, pl.ds(p, 1), :],
                pltpu.roll(face[k], rows - 1, 0),
            )
            res[k, p] = 0.5 * (
                (flux_stream[k, p + 1] - flux_stream[k, p]) + (over - face[k]) + res[k, p]
            )
        return carry

    lax.fori_loop(0, planes, plane_residual, 0)
    def plane_drive(p, previous):
        term = half_apply(half_jacobian(get(prim, (p,), 7)), previous, 1.0)
        out = mat_vec(lambda e: diag[e, p], [term[k] - res[k, p] for k in range(5)])
        put(drive, (p,), out)
        return tuple(out)

    current = mat_vec(lambda e: diag[e, 0], [-res[k, 0] for k in range(5)])
    put(drive, (0,), current)
    current = lax.fori_loop(1, planes, plane_drive, tuple(current))
    current = half_apply(half_jacobian(get(prim, (planes,), 7)), current, 1.0)
    for k in range(5):
        pack(a_out, k, current[k])

    @pl.when(me < last)
    def _():
        send_some(VEC_F, 1, streams)

    keep_own(MAT_F)
    keep_own(VEC_F)
    lax.fori_loop(0, planes - 1, matrices_b, 0)
    lax.fori_loop(0, 5, product_b, 0)
    keep_own(MAT_B)
    half = streams // 2

    @pl.when(inner)
    def _():
        sent(MAT_F)
        send_some(MAT_B, 1, half)

    gather(MAT_F, 1, last)
    gather(VEC_F, 0, last)
    current = [a_in[0, k] for k in range(5)]
    for j in range(1, streams):
        for k in range(5):
            s_out[j, k] = current[k]
        if j < last:
            step = mat_vec(lambda e: p_in[j, e], current)
            current = [a_in[j, k] + step[k] for k in range(5)]
    hand_back(BACK_F, 0)

    @pl.when(inner)
    def _():
        send_some(MAT_B, half, streams)

    def joined(into, k):
        wide = []
        for c in range(chunks):
            parts = [into[c * per_chunk + i, k] for i in range(per_chunk)]
            wide.append(parts[0] if per_chunk == 1 else jnp.concatenate(parts, axis=0))
        return wide[0] if chunks == 1 else jnp.concatenate(wide, axis=1)

    @pl.when(me > 0)
    def _():
        gather(BACK_F, 0, streams)

    delta = [jnp.where(me == 0, 0.0, joined(s_in, k)) for k in range(5)]
    for p in range(planes):
        delta = mat_vec(lambda e: diag[e, 0] if p == 0 else mats_f[e, p], delta)
        current = [drive[k, p] + delta[k] for k in range(5)]
        put(base, (p,), current)
    for p in reversed(range(planes - 1)):
        step = mat_vec(lambda e: mats_b[e, p], current)
        current = [base[k, p] + step[k] for k in range(5)]
        put(base, (p,), current)
    current = half_apply(half_jacobian(get(prim, (1,), 7)), current, -1.0)
    for k in range(5):
        pack(b_out, k, current[k])

    @pl.when(me > 0)
    def _():
        send_some(VEC_B, 1, streams)

    keep_own(VEC_B)

    gather(MAT_B, 1, last)
    gather(VEC_B, 1, streams)
    current = [b_in[last, k] for k in range(5)]
    for j in reversed(range(last)):
        for k in range(5):
            u_out[j, k] = current[k]
        if j > 0:
            step = mat_vec(lambda e: q_in[j, e], current)
            current = [b_in[j, k] + step[k] for k in range(5)]
    hand_back(BACK_B, last)

    @pl.when(me < last)
    def _():
        gather(BACK_B, 0, streams)

    delta = [jnp.where(me == last, 0.0, joined(u_in, k)) for k in range(5)]
    for p in reversed(range(planes)):
        if p == planes - 1:
            delta = [-d for d in mat_vec(lambda e: diag[e, p], delta)]
        else:
            delta = mat_vec(lambda e: mats_b[e, p], delta)
        for k in range(5):
            upd[k, p] = base[k, p] + delta[k]

    for copy in halos:
        copy.wait_send()

    @pl.when(inner)
    def _():
        sent(MAT_B)

    @pl.when(me < last)
    def _():
        sent(VEC_F)

    @pl.when(me > 0)
    def _():
        sent(VEC_B)

    def sent_back(t, carry):
        @pl.when(t != me)
        def _():
            outgoing(BACK_F, t).wait_send()

        @pl.when(t - 1 != me)
        def _():
            outgoing(BACK_B, t - 1).wait_send()

        return carry

    lax.fori_loop(1, streams, sent_back, 0)


def local(streams, crosses, state, diag, kinds_low, kinds_high):
    _, planes, rows, lanes = state.shape
    piece = rows * (lanes // CHUNK) // streams
    f32 = jnp.float32
    block = (planes, rows, lanes)

    def vmem(*shape):
        return pltpu.VMEM(shape, f32)

    return pl.pallas_call(
        functools.partial(kernel, streams, crosses),
        out_shape=[jax.ShapeDtypeStruct(state.shape, f32)] * 2,
        in_specs=[pl.BlockSpec(memory_space=pltpu.HBM)] * 3,
        out_specs=[pl.BlockSpec(memory_space=pltpu.VMEM)] * 2,
        scratch_shapes=[
            vmem(5, *block),
            vmem(25, *block),
            pltpu.VMEM((planes, lanes), jnp.int32),
            vmem(7, planes + 2, rows, lanes),
            vmem(2, 5, planes, lanes),
            vmem(2, 5, planes, lanes),
            vmem(2, 5, rows, lanes),
            vmem(7, planes, lanes),
            vmem(5, planes, lanes),
            vmem(5, planes + 1, rows, lanes),
            vmem(5, *block),
            vmem(25, *block),
            vmem(25, *block),
            vmem(5, *block),
            *[vmem(streams, 25, piece, CHUNK)] * 4,
            *[vmem(streams, 5, piece, CHUNK)] * 8,
            pltpu.SemaphoreType.DMA((3,)),
            pltpu.SemaphoreType.DMA((4,)),
            pltpu.SemaphoreType.DMA((4,)),
            pltpu.SemaphoreType.DMA((6, streams)),
            pltpu.SemaphoreType.DMA((6, streams)),
        ],
        compiler_params=pltpu.CompilerParams(
            collective_id=0, has_side_effects=True, vmem_limit_bytes=54400 * 1024
        ),
        cost_estimate=pl.CostEstimate(
            flops=16000000, bytes_accessed=2700000, transcendentals=100000
        ),
    )(state, diag, kinds_low + 4 * kinds_high)


def solution(mesh):
    spec = P(None, "stream", "cross", None)
    return jax.shard_map(
        functools.partial(local, mesh.shape["stream"], mesh.shape["cross"]),
        mesh=mesh,
        in_specs=(spec, spec, P("stream", None), P("stream", None)),
        out_specs=(spec, spec),
        check_vma=False,
    )
```

```python
import functools

import jax
import jax.numpy as jnp
from jax import lax
from jax.experimental import pallas as pl
from jax.experimental.pallas import tpu as pltpu
from jax.sharding import PartitionSpec as P

MESH = pl.DeviceIdType.MESH
free_values = (1.0, 0.0, 0.0, 0.0, 2.5)
CHUNK = 128
RHO, U1, U2, U3, PRES, ENTH, ROOT = range(7)


def primitive(q):
    inv_root = lax.rsqrt(q[0])
    inv = inv_root * inv_root
    u = [q[1] * inv, q[2] * inv, q[3] * inv]
    pressure = 0.4 * (q[4] - 0.5 * (q[1] * u[0] + q[2] * u[1] + q[3] * u[2]))
    return [q[0], *u, pressure, (q[4] + pressure) * inv, q[0] * inv_root]


def roe_twice(left, right, d):
    share = right[ROOT] / (left[ROOT] + right[ROOT])
    jump = [right[1 + k] - left[1 + k] for k in range(3)]
    avg = [left[1 + k] + share * jump[k] for k in range(3)]
    enth = left[ENTH] + share * (right[ENTH] - left[ENTH])
    kinetic = 0.5 * (avg[0] * avg[0] + avg[1] * avg[1] + avg[2] * avg[2])
    sound_sq = 0.4 * (enth - kinetic)
    inv_sound = lax.rsqrt(sound_sq)
    sound = sound_sq * inv_sound
    inv_sq = inv_sound * inv_sound
    dens = left[ROOT] * right[ROOT]
    normal = avg[d]
    scaled_pres = (right[PRES] - left[PRES]) * inv_sq
    scaled_jump = dens * inv_sound * jump[d]
    slow = jnp.abs(normal - sound) * (0.5 * (scaled_pres - scaled_jump))
    fast = jnp.abs(normal + sound) * (0.5 * (scaled_pres + scaled_jump))
    speed = jnp.abs(normal)
    entropy = speed * (right[RHO] - left[RHO] - scaled_pres)
    shear = speed * dens
    acoustic = slow + fast
    total = acoustic + entropy
    spread = (fast - slow) * sound
    mass_left = left[RHO] * left[1 + d]
    mass_right = right[RHO] * right[1 + d]
    pieces = [mass_left + mass_right - total]
    along = 0.0
    for k in range(3):
        central = mass_left * left[1 + k] + mass_right * right[1 + k]
        if k == d:
            pieces.append(central + (left[PRES] + right[PRES]) - (total * avg[k] + spread))
        else:
            pieces.append(central - (total * avg[k] + shear * jump[k]))
            along = along + avg[k] * jump[k]
    pieces.append(
        mass_left * left[ENTH]
        + mass_right * right[ENTH]
        - (acoustic * enth + spread * normal + entropy * kinetic + shear * along)
    )
    return pieces


def half_jacobian(w):
    u, v, s = 0.5 * w[U1], 0.5 * w[U2], 0.5 * w[U3]
    phi = 0.1 * (w[U1] * w[U1] + w[U2] * w[U2] + w[U3] * w[U3])
    inv_root = w[ROOT] / w[RHO]
    pos = 1.4 * w[PRES]
    lam = jnp.abs(u) + 0.5 * (pos * lax.rsqrt(pos) * inv_root)
    return u, v, s, phi, 0.5 * w[ENTH], lam, w[U1], w[U2], w[U3]


def row_times(row, jac, sign):
    u, v, s, phi, enth, lam, u1, _, _ = jac
    pres = row[1] + u1 * row[4]
    move = u * row[1] + v * row[2] + s * row[3] + enth * row[4]
    own = u + sign * lam
    return [
        phi * pres - u1 * move + (sign * lam) * row[0],
        0.5 * row[0] + own * row[1] + move - 0.4 * (u * pres),
        own * row[2] - 0.4 * (v * pres),
        own * row[3] - 0.4 * (s * pres),
        own * row[4] + 0.2 * pres,
    ]


def half_apply(jac, vec, sign):
    u, v, s, phi, enth, lam, u1, _, _ = jac
    own = u + sign * lam
    q = vec[1] - u1 * vec[0]
    pres = phi * vec[0] - 0.4 * (u * vec[1] + v * vec[2] + s * vec[3]) + 0.2 * vec[4]
    return [
        0.5 * vec[1] + (sign * lam) * vec[0],
        own * vec[1] + u * q + pres,
        own * vec[2] + v * q,
        own * vec[3] + s * q,
        own * vec[4] + u1 * pres + enth * q,
    ]


def mat_vec(load, vec):
    out = []
    for r in range(5):
        term = [load(5 * r + k) * vec[k] for k in range(5)]
        out.append((term[0] + term[1]) + (term[2] + term[3]) + term[4])
    return out


def kernel(
    streams, crosses,
    state_hbm, diag_hbm, kinds_hbm, res, upd,
    state, diag, kinds, prim, edge, halo_cross, halo_stream, low_prim, top_flux,
    flux_stream, drive, mats_f, mats_b, base,
    p_out, p_in, q_out, q_in, a_out, a_in, s_out, s_in, b_out, b_in, u_out, u_in,
    passed, load_sem, halo_send, halo_recv, sends, recvs, first_recv, second_send,
):
    me = lax.axis_index("stream")
    mine = lax.axis_index("cross")
    planes, rows, lanes = state.shape[1:]
    chunks = lanes // CHUNK
    piece = rows * chunks // streams
    per_chunk = rows // piece
    last = streams - 1
    up = {"stream": lax.rem(me + 1, streams)}
    down = {"stream": lax.rem(me + last, streams)}
    high = {"cross": lax.rem(mine + 1, crosses)}
    low = {"cross": lax.rem(mine + crosses - 1, crosses)}

    loads = [
        pltpu.make_async_copy(src, dst, load_sem.at[i])
        for i, (src, dst) in enumerate(
            [(state_hbm, state), (diag_hbm, diag), (kinds_hbm, kinds)]
        )
    ]
    for copy in loads:
        copy.start()
    barrier = pltpu.get_barrier_semaphore()

    def greet(o, carry):
        pl.semaphore_signal(
            barrier, inc=1, device_id={"stream": lax.rem(me + o, streams)}, device_id_type=MESH
        )
        return carry

    lax.fori_loop(1, streams, greet, 0)
    for to in (high, low):
        pl.semaphore_signal(barrier, inc=1, device_id=to, device_id_type=MESH)

    def get(ref, index, count):
        return [ref[(k, *index)] for k in range(count)]

    def put(ref, index, values):
        for k, value in enumerate(values):
            ref[(k, *index)] = value

    def pack(out, e, value):
        for c in range(chunks):
            for i in range(per_chunk):
                out[c * per_chunk + i, e] = value[
                    i * piece : (i + 1) * piece, c * CHUNK : (c + 1) * CHUNK
                ]

    def matrices_f(p, carry):
        jac = half_jacobian(get(prim, (p,), 7))
        for r in range(5):
            row = [diag[5 * r + k, p] for k in range(5)]
            for k, value in enumerate(row_times(row, jac, 1.0)):
                mats_f[5 * r + k, p] = value
        return carry

    def matrices_b(p, carry):
        jac = half_jacobian(get(prim, (p + 2,), 7))
        for r in range(5):
            row = [-diag[5 * r + k, p] for k in range(5)]
            for k, value in enumerate(row_times(row, jac, -1.0)):
                mats_b[5 * r + k, p] = value
        return carry

    def product_f(j, carry):
        vec = [diag[5 * k + j, 0] for k in range(5)]
        for p in range(1, planes):
            vec = mat_vec(lambda e: mats_f[e, p], vec)
        vec = half_apply(half_jacobian(get(prim, (planes,), 7)), vec, 1.0)
        for r in range(5):
            pack(p_out, 5 * r + j, vec[r])
        return carry

    def product_b(j, carry):
        vec = [-diag[5 * k + j, planes - 1] for k in range(5)]
        for p in reversed(range(planes - 1)):
            vec = mat_vec(lambda e: mats_b[e, p], vec)
        vec = half_apply(half_jacobian(get(prim, (1,), 7)), vec, -1.0)
        for r in range(5):
            pack(q_out, 5 * r + j, vec[r])
        return carry

    def own_plane(p, carry):
        put(prim, (p + 1,), primitive(get(state, (p,), 5)))
        return carry

    loads[0].wait()
    for p in range(planes):
        for k in range(5):
            edge[0, k, pl.ds(p, 1), :] = state[k, p, pl.ds(0, 1), :]
            edge[1, k, pl.ds(p, 1), :] = state[k, p, pl.ds(rows - 1, 1), :]
    lax.fori_loop(0, planes, own_plane, 0)
    loads[1].wait()
    lax.fori_loop(1, planes, matrices_f, 0)
    lax.fori_loop(0, 5, product_f, 0)
    pl.semaphore_wait(barrier, streams + 1)

    def remote(src, dst, send, recv, to):
        return pltpu.make_async_remote_copy(
            src_ref=src, dst_ref=dst, send_sem=send, recv_sem=recv,
            device_id=to, device_id_type=MESH,
        )

    halos = [
        remote(state.at[:, planes - 1], halo_stream.at[0], halo_send.at[0], halo_recv.at[0], up),
        remote(state.at[:, 0], halo_stream.at[1], halo_send.at[1], halo_recv.at[1], down),
        remote(edge.at[1], halo_cross.at[0], halo_send.at[2], halo_recv.at[2], high),
        remote(edge.at[0], halo_cross.at[1], halo_send.at[3], halo_recv.at[3], low),
    ]
    for copy in halos:
        copy.start()

    boxes = [
        (p_out, p_in), (a_out, a_in), (s_out, s_in), (q_out, q_in), (b_out, b_in), (u_out, u_in)
    ]
    MAT_F, VEC_F, BACK_F, MAT_B, VEC_B, BACK_B = range(6)

    def outgoing(kind, to):
        out, into = boxes[kind]
        return remote(
            out.at[to], into.at[me], sends.at[kind, to], recvs.at[kind, me], {"stream": to}
        )

    def wait_from(kind, source):
        out, into = boxes[kind]

        @pl.when(source != me)
        def _():
            remote(
                out.at[source], into.at[source], sends.at[kind, source],
                recvs.at[kind, source], {"stream": source},
            ).wait_recv()

    def send_some(kind, first, end):
        def one(o, carry):
            outgoing(kind, lax.rem(me + o, streams)).start()
            return carry

        lax.fori_loop(first, end, one, 0)

    def sent(kind):
        def one(o, carry):
            outgoing(kind, lax.rem(me + o, streams)).wait_send()
            return carry

        lax.fori_loop(1, streams, one, 0)

    def keep_own(kind):
        out, into = boxes[kind]
        into[me] = out[me]

    inner = (me > 0) & (me < last)

    ring = streams // 2
    corner = ring // 4

    def around(by):
        return (me // ring) * ring + lax.rem(lax.rem(me, ring) + by, ring)

    def first_leg(kind, way):
        to = lax.rem(me + (ring // 2, streams - ring // 2)[way], streams)
        middle = around((corner, ring - corner)[way])
        slot = (kind // 3) * 2 + way
        return remote(
            boxes[kind][0].at[to], passed.at[slot], sends.at[kind, to], first_recv.at[slot],
            {"stream": middle},
        )

    def second_leg(kind, way):
        origin = around((ring - corner, corner)[way])
        to = lax.rem(origin + (ring // 2, streams - ring // 2)[way], streams)
        slot = (kind // 3) * 2 + way
        return origin, remote(
            passed.at[slot], boxes[kind][1].at[origin], second_send.at[slot],
            recvs.at[kind, origin], {"stream": to},
        )

    def start_first(kind):
        for way in range(2):
            first_leg(kind, way).start()

    def pass_on(kind):
        for way in range(2):
            origin, copy = second_leg(kind, way)

            @pl.when((origin > 0) & (origin < last))
            def _():
                first_leg(kind, way).wait_recv()
                copy.start()

    def passed_on(kind):
        for way in range(2):
            origin, copy = second_leg(kind, way)

            @pl.when((origin > 0) & (origin < last))
            def _():
                copy.wait_send()

    def send_matrices(kind, first, end):
        def one(o, carry):
            @pl.when(lax.rem(o, ring) != ring // 2)
            def _():
                outgoing(kind, lax.rem(me + o, streams)).start()

            return carry

        lax.fori_loop(first, end, one, 0)

    @pl.when(inner)
    def _():
        start_first(MAT_F)
        send_matrices(MAT_F, 1, streams)

    def inner_face(f, carry):
        put(flux_stream, (f,), roe_twice(get(prim, (f,), 7), get(prim, (f + 1,), 7), 0))
        return carry

    def span_plane(p, carry):
        cell = get(prim, (p + 1,), 7)
        ahead = [pltpu.roll(field, lanes - 1, 1) for field in cell]
        face = roe_twice(cell, ahead, 2)
        put(res, (p,), [f - pltpu.roll(f, 1, 1) for f in face])
        return carry

    lax.fori_loop(0, planes, span_plane, 0)
    lax.fori_loop(1, planes, inner_face, 0)
    halos[0].wait_recv()
    halos[1].wait_recv()
    below = [jnp.where(me == 0, free_values[k], halo_stream[0, k]) for k in range(5)]
    put(prim, (0,), primitive(below))
    above = [
        jnp.where(me == last, state[k, planes - 1], halo_stream[1, k]) for k in range(5)
    ]
    put(prim, (planes + 1,), primitive(above))
    lax.fori_loop(0, 2, lambda i, c: inner_face(i * planes, c), 0)
    pass_on(MAT_F)
    halos[2].wait_recv()
    halos[3].wait_recv()
    loads[2].wait()

    def ghost(cell, kinds):
        out = []
        for k in range(5):
            mirror = -cell[k] if k == 2 else cell[k]
            out.append(
                jnp.where(kinds == 0, mirror, jnp.where(kinds == 1, cell[k], free_values[k]))
            )
        return out

    row_first = [edge[0, k] for k in range(5)]
    row_last = [edge[1, k] for k in range(5)]
    ghost_low = ghost(row_first, kinds[...] & 3)
    ghost_high = ghost(row_last, kinds[...] >> 2)
    side_low = [jnp.where(mine == 0, ghost_low[k], halo_cross[0, k]) for k in range(5)]
    side_high = [
        jnp.where(mine == crosses - 1, ghost_high[k], halo_cross[1, k]) for k in range(5)
    ]
    put(low_prim, (), primitive(side_low))
    put(top_flux, (), roe_twice(primitive(row_last), primitive(side_high), 1))

    row_no = lax.broadcasted_iota(jnp.int32, (rows, lanes), 0)

    def plane_residual(p, carry):
        cell = get(prim, (p + 1,), 7)
        under = [
            jnp.where(row_no == 0, low_prim[k, pl.ds(p, 1), :], pltpu.roll(cell[k], 1, 0))
            for k in range(7)
        ]
        face = roe_twice(under, cell, 1)
        for k in range(5):
            over = jnp.where(
                row_no == rows - 1,
                top_flux[k, pl.ds(p, 1), :],
                pltpu.roll(face[k], rows - 1, 0),
            )
            res[k, p] = 0.5 * (
                (flux_stream[k, p + 1] - flux_stream[k, p]) + (over - face[k]) + res[k, p]
            )
        return carry

    lax.fori_loop(0, planes, plane_residual, 0)
    def plane_drive(p, previous):
        term = half_apply(half_jacobian(get(prim, (p,), 7)), previous, 1.0)
        out = mat_vec(lambda e: diag[e, p], [term[k] - res[k, p] for k in range(5)])
        put(drive, (p,), out)
        return tuple(out)

    current = mat_vec(lambda e: diag[e, 0], [-res[k, 0] for k in range(5)])
    put(drive, (0,), current)
    current = lax.fori_loop(1, planes, plane_drive, tuple(current))
    current = half_apply(half_jacobian(get(prim, (planes,), 7)), current, 1.0)
    for k in range(5):
        pack(a_out, k, current[k])

    @pl.when(me < last)
    def _():
        send_some(VEC_F, 1, streams)

    keep_own(MAT_F)
    keep_own(VEC_F)
    lax.fori_loop(0, planes - 1, matrices_b, 0)
    lax.fori_loop(0, 5, product_b, 0)
    keep_own(MAT_B)
    half = streams // 2

    @pl.when(inner)
    def _():
        sent(MAT_F)
        start_first(MAT_B)
        send_matrices(MAT_B, 1, half - 1)

    def hand_back(kind, to, values):
        out, into = boxes[kind]
        for k in range(5):
            out[to, k] = values[k]

        @pl.when(to != me)
        def _():
            outgoing(kind, to).start()

        @pl.when(to == me)
        def _():
            for k in range(5):
                into[me, k] = values[k]

    wait_from(VEC_F, 0)
    current = [a_in[0, k] for k in range(5)]
    hand_back(BACK_F, 1, current)

    def scan_f(j, vec):
        wait_from(MAT_F, j)
        wait_from(VEC_F, j)
        step = mat_vec(lambda e: p_in[j, e], vec)
        out = [a_in[j, k] + step[k] for k in range(5)]
        hand_back(BACK_F, j + 1, out)
        return tuple(out)

    lax.fori_loop(1, last, scan_f, tuple(current))

    pass_on(MAT_B)

    @pl.when(inner)
    def _():
        send_matrices(MAT_B, half - 1, streams)

    def gather(kind):
        def one(j, carry):
            wait_from(kind, j)
            return carry

        lax.fori_loop(0, streams, one, 0)

    def joined(into, k):
        wide = []
        for c in range(chunks):
            parts = [into[c * per_chunk + i, k] for i in range(per_chunk)]
            wide.append(parts[0] if per_chunk == 1 else jnp.concatenate(parts, axis=0))
        return wide[0] if chunks == 1 else jnp.concatenate(wide, axis=1)

    @pl.when(me > 0)
    def _():
        gather(BACK_F)

    delta = [jnp.where(me == 0, 0.0, joined(s_in, k)) for k in range(5)]
    for p in range(planes):
        delta = mat_vec(lambda e: diag[e, 0] if p == 0 else mats_f[e, p], delta)
        current = [drive[k, p] + delta[k] for k in range(5)]
        put(base, (p,), current)
    for p in reversed(range(planes - 1)):
        step = mat_vec(lambda e: mats_b[e, p], current)
        current = [base[k, p] + step[k] for k in range(5)]
        put(base, (p,), current)
    current = half_apply(half_jacobian(get(prim, (1,), 7)), current, -1.0)
    for k in range(5):
        pack(b_out, k, current[k])

    @pl.when(me > 0)
    def _():
        send_some(VEC_B, 1, streams)

    keep_own(VEC_B)

    wait_from(VEC_B, last)
    current = [b_in[last, k] for k in range(5)]
    hand_back(BACK_B, last - 1, current)

    def scan_b(n, vec):
        j = last - n
        wait_from(MAT_B, j)
        wait_from(VEC_B, j)
        step = mat_vec(lambda e: q_in[j, e], vec)
        out = [b_in[j, k] + step[k] for k in range(5)]
        hand_back(BACK_B, j - 1, out)
        return tuple(out)

    lax.fori_loop(1, last, scan_b, tuple(current))

    @pl.when(me < last)
    def _():
        gather(BACK_B)

    delta = [jnp.where(me == last, 0.0, joined(u_in, k)) for k in range(5)]
    for p in reversed(range(planes)):
        if p == planes - 1:
            delta = [-d for d in mat_vec(lambda e: diag[e, p], delta)]
        else:
            delta = mat_vec(lambda e: mats_b[e, p], delta)
        for k in range(5):
            upd[k, p] = base[k, p] + delta[k]

    for copy in halos:
        copy.wait_send()

    @pl.when(inner)
    def _():
        sent(MAT_B)

    passed_on(MAT_F)
    passed_on(MAT_B)

    @pl.when(me < last)
    def _():
        sent(VEC_F)

    @pl.when(me > 0)
    def _():
        sent(VEC_B)

    def sent_back(t, carry):
        @pl.when(t != me)
        def _():
            outgoing(BACK_F, t).wait_send()

        @pl.when(t - 1 != me)
        def _():
            outgoing(BACK_B, t - 1).wait_send()

        return carry

    lax.fori_loop(1, streams, sent_back, 0)


def local(streams, crosses, state, diag, kinds_low, kinds_high):
    _, planes, rows, lanes = state.shape
    piece = rows * (lanes // CHUNK) // streams
    f32 = jnp.float32
    block = (planes, rows, lanes)

    def vmem(*shape):
        return pltpu.VMEM(shape, f32)

    return pl.pallas_call(
        functools.partial(kernel, streams, crosses),
        out_shape=[jax.ShapeDtypeStruct(state.shape, f32)] * 2,
        in_specs=[pl.BlockSpec(memory_space=pltpu.HBM)] * 3,
        out_specs=[pl.BlockSpec(memory_space=pltpu.VMEM)] * 2,
        scratch_shapes=[
            vmem(5, *block),
            vmem(25, *block),
            pltpu.VMEM((planes, lanes), jnp.int32),
            vmem(7, planes + 2, rows, lanes),
            vmem(2, 5, planes, lanes),
            vmem(2, 5, planes, lanes),
            vmem(2, 5, rows, lanes),
            vmem(7, planes, lanes),
            vmem(5, planes, lanes),
            vmem(5, planes + 1, rows, lanes),
            vmem(5, *block),
            vmem(25, *block),
            vmem(25, *block),
            vmem(5, *block),
            *[vmem(streams, 25, piece, CHUNK)] * 4,
            *[vmem(streams, 5, piece, CHUNK)] * 8,
            vmem(4, 25, piece, CHUNK),
            pltpu.SemaphoreType.DMA((3,)),
            pltpu.SemaphoreType.DMA((4,)),
            pltpu.SemaphoreType.DMA((4,)),
            pltpu.SemaphoreType.DMA((6, streams)),
            pltpu.SemaphoreType.DMA((6, streams)),
            pltpu.SemaphoreType.DMA((4,)),
            pltpu.SemaphoreType.DMA((4,)),
        ],
        compiler_params=pltpu.CompilerParams(
            collective_id=0, has_side_effects=True, vmem_limit_bytes=54400 * 1024
        ),
        cost_estimate=pl.CostEstimate(
            flops=16000000, bytes_accessed=2700000, transcendentals=100000
        ),
    )(state, diag, kinds_low + 4 * kinds_high)


def solution(mesh):
    spec = P(None, "stream", "cross", None)
    return jax.shard_map(
        functools.partial(local, mesh.shape["stream"], mesh.shape["cross"]),
        mesh=mesh,
        in_specs=(spec, spec, P("stream", None), P("stream", None)),
        out_specs=(spec, spec),
        check_vma=False,
    )
```

```python
import functools

import jax
import jax.numpy as jnp
from jax import lax
from jax.experimental import pallas as pl
from jax.experimental.pallas import tpu as pltpu
from jax.sharding import PartitionSpec as P

MESH = pl.DeviceIdType.MESH
free_values = (1.0, 0.0, 0.0, 0.0, 2.5)
CHUNK = 128
RHO, U1, U2, U3, PRES, ENTH, ROOT = range(7)


def primitive(q):
    inv_root = lax.rsqrt(q[0])
    inv = inv_root * inv_root
    u = [q[1] * inv, q[2] * inv, q[3] * inv]
    pressure = 0.4 * (q[4] - 0.5 * (q[1] * u[0] + q[2] * u[1] + q[3] * u[2]))
    return [q[0], *u, pressure, (q[4] + pressure) * inv, q[0] * inv_root]


def roe_twice(left, right, d):
    share = right[ROOT] / (left[ROOT] + right[ROOT])
    jump = [right[1 + k] - left[1 + k] for k in range(3)]
    avg = [left[1 + k] + share * jump[k] for k in range(3)]
    enth = left[ENTH] + share * (right[ENTH] - left[ENTH])
    kinetic = 0.5 * (avg[0] * avg[0] + avg[1] * avg[1] + avg[2] * avg[2])
    sound_sq = 0.4 * (enth - kinetic)
    inv_sound = lax.rsqrt(sound_sq)
    sound = sound_sq * inv_sound
    inv_sq = inv_sound * inv_sound
    dens = left[ROOT] * right[ROOT]
    normal = avg[d]
    scaled_pres = (right[PRES] - left[PRES]) * inv_sq
    scaled_jump = dens * inv_sound * jump[d]
    slow = jnp.abs(normal - sound) * (0.5 * (scaled_pres - scaled_jump))
    fast = jnp.abs(normal + sound) * (0.5 * (scaled_pres + scaled_jump))
    speed = jnp.abs(normal)
    entropy = speed * (right[RHO] - left[RHO] - scaled_pres)
    shear = speed * dens
    acoustic = slow + fast
    total = acoustic + entropy
    spread = (fast - slow) * sound
    mass_left = left[RHO] * left[1 + d]
    mass_right = right[RHO] * right[1 + d]
    pieces = [mass_left + mass_right - total]
    along = 0.0
    for k in range(3):
        central = mass_left * left[1 + k] + mass_right * right[1 + k]
        if k == d:
            pieces.append(central + (left[PRES] + right[PRES]) - (total * avg[k] + spread))
        else:
            pieces.append(central - (total * avg[k] + shear * jump[k]))
            along = along + avg[k] * jump[k]
    pieces.append(
        mass_left * left[ENTH]
        + mass_right * right[ENTH]
        - (acoustic * enth + spread * normal + entropy * kinetic + shear * along)
    )
    return pieces


def half_jacobian(w):
    u, v, s = 0.5 * w[U1], 0.5 * w[U2], 0.5 * w[U3]
    phi = 0.1 * (w[U1] * w[U1] + w[U2] * w[U2] + w[U3] * w[U3])
    inv_root = w[ROOT] / w[RHO]
    pos = 1.4 * w[PRES]
    lam = jnp.abs(u) + 0.5 * (pos * lax.rsqrt(pos) * inv_root)
    return u, v, s, phi, 0.5 * w[ENTH], lam, w[U1], w[U2], w[U3]


def row_times(row, jac, sign):
    u, v, s, phi, enth, lam, u1, _, _ = jac
    pres = row[1] + u1 * row[4]
    move = u * row[1] + v * row[2] + s * row[3] + enth * row[4]
    own = u + sign * lam
    return [
        phi * pres - u1 * move + (sign * lam) * row[0],
        0.5 * row[0] + own * row[1] + move - 0.4 * (u * pres),
        own * row[2] - 0.4 * (v * pres),
        own * row[3] - 0.4 * (s * pres),
        own * row[4] + 0.2 * pres,
    ]


def half_apply(jac, vec, sign):
    u, v, s, phi, enth, lam, u1, _, _ = jac
    own = u + sign * lam
    q = vec[1] - u1 * vec[0]
    pres = phi * vec[0] - 0.4 * (u * vec[1] + v * vec[2] + s * vec[3]) + 0.2 * vec[4]
    return [
        0.5 * vec[1] + (sign * lam) * vec[0],
        own * vec[1] + u * q + pres,
        own * vec[2] + v * q,
        own * vec[3] + s * q,
        own * vec[4] + u1 * pres + enth * q,
    ]


def mat_vec(load, vec):
    out = []
    for r in range(5):
        term = [load(5 * r + k) * vec[k] for k in range(5)]
        out.append((term[0] + term[1]) + (term[2] + term[3]) + term[4])
    return out


def kernel(
    streams, crosses,
    state_hbm, diag_hbm, kinds_hbm, res, upd,
    state, diag, kinds, prim, edge, halo_cross, halo_stream, low_prim, top_flux,
    flux_stream, drive, mats_f, mats_b, base, back,
    p_out, p_in, q_out, q_in, a_out, a_in, s_out, s_in, b_out, b_in, u_out, u_in,
    load_sem, halo_send, halo_recv, sends, recvs,
):
    me = lax.axis_index("stream")
    mine = lax.axis_index("cross")
    planes, rows, lanes = state.shape[1:]
    chunks = lanes // CHUNK
    piece = rows * chunks // streams
    per_chunk = rows // piece
    last = streams - 1
    up = {"stream": lax.rem(me + 1, streams)}
    down = {"stream": lax.rem(me + last, streams)}
    high = {"cross": lax.rem(mine + 1, crosses)}
    low = {"cross": lax.rem(mine + crosses - 1, crosses)}

    loads = [
        pltpu.make_async_copy(src, dst, load_sem.at[i])
        for i, (src, dst) in enumerate(
            [(state_hbm, state), (diag_hbm, diag), (kinds_hbm, kinds)]
        )
    ]
    for copy in loads:
        copy.start()
    barrier = pltpu.get_barrier_semaphore()

    def greet(o, carry):
        pl.semaphore_signal(
            barrier, inc=1, device_id={"stream": lax.rem(me + o, streams)}, device_id_type=MESH
        )
        return carry

    lax.fori_loop(1, streams, greet, 0)
    for to in (high, low):
        pl.semaphore_signal(barrier, inc=1, device_id=to, device_id_type=MESH)

    def get(ref, index, count):
        return [ref[(k, *index)] for k in range(count)]

    def put(ref, index, values):
        for k, value in enumerate(values):
            ref[(k, *index)] = value

    def pack(out, e, value):
        for c in range(chunks):
            for i in range(per_chunk):
                out[c * per_chunk + i, e] = value[
                    i * piece : (i + 1) * piece, c * CHUNK : (c + 1) * CHUNK
                ]

    def matrices_f(p, carry):
        jac = half_jacobian(get(prim, (p,), 7))
        for r in range(5):
            row = [diag[5 * r + k, p] for k in range(5)]
            for k, value in enumerate(row_times(row, jac, 1.0)):
                mats_f[5 * r + k, p] = value
        return carry

    def matrices_b(p, carry):
        jac = half_jacobian(get(prim, (p + 2,), 7))
        for r in range(5):
            row = [-diag[5 * r + k, p] for k in range(5)]
            for k, value in enumerate(row_times(row, jac, -1.0)):
                mats_b[5 * r + k, p] = value
        return carry

    def product_f(j, carry):
        vec = [diag[5 * k + j, 0] for k in range(5)]
        for p in range(1, planes):
            vec = mat_vec(lambda e: mats_f[e, p], vec)
        vec = half_apply(half_jacobian(get(prim, (planes,), 7)), vec, 1.0)
        for r in range(5):
            pack(p_out, 5 * r + j, vec[r])
        return carry

    def product_b(j, carry):
        vec = [-diag[5 * k + j, planes - 1] for k in range(5)]
        for p in reversed(range(planes - 1)):
            vec = mat_vec(lambda e: mats_b[e, p], vec)
        vec = half_apply(half_jacobian(get(prim, (1,), 7)), vec, -1.0)
        for r in range(5):
            pack(q_out, 5 * r + j, vec[r])
        return carry

    def own_plane(p, carry):
        put(prim, (p + 1,), primitive(get(state, (p,), 5)))
        return carry

    loads[0].wait()
    for p in range(planes):
        for k in range(5):
            edge[0, k, pl.ds(p, 1), :] = state[k, p, pl.ds(0, 1), :]
            edge[1, k, pl.ds(p, 1), :] = state[k, p, pl.ds(rows - 1, 1), :]
    lax.fori_loop(0, planes, own_plane, 0)
    loads[1].wait()
    lax.fori_loop(1, planes, matrices_f, 0)
    lax.fori_loop(0, 5, product_f, 0)
    pl.semaphore_wait(barrier, streams + 1)

    def remote(src, dst, send, recv, to):
        return pltpu.make_async_remote_copy(
            src_ref=src, dst_ref=dst, send_sem=send, recv_sem=recv,
            device_id=to, device_id_type=MESH,
        )

    halos = [
        remote(state.at[:, planes - 1], halo_stream.at[0], halo_send.at[0], halo_recv.at[0], up),
        remote(state.at[:, 0], halo_stream.at[1], halo_send.at[1], halo_recv.at[1], down),
        remote(edge.at[1], halo_cross.at[0], halo_send.at[2], halo_recv.at[2], high),
        remote(edge.at[0], halo_cross.at[1], halo_send.at[3], halo_recv.at[3], low),
    ]
    for copy in halos:
        copy.start()

    boxes = [
        (p_out, p_in), (a_out, a_in), (s_out, s_in), (q_out, q_in), (b_out, b_in), (u_out, u_in)
    ]
    MAT_F, VEC_F, BACK_F, MAT_B, VEC_B, BACK_B = range(6)

    def outgoing(kind, to):
        out, into = boxes[kind]
        return remote(
            out.at[to], into.at[me], sends.at[kind, to], recvs.at[kind, me], {"stream": to}
        )

    def wait_from(kind, source):
        out, into = boxes[kind]

        @pl.when(source != me)
        def _():
            remote(
                out.at[source], into.at[source], sends.at[kind, source],
                recvs.at[kind, source], {"stream": source},
            ).wait_recv()

    ring = streams // 2
    offsets = sorted(range(1, streams), key=lambda o: -min(o % ring, ring - o % ring))

    def send_some(kind, first, end):
        for o in offsets[first:end]:
            outgoing(kind, lax.rem(me + o, streams)).start()

    def sent(kind):
        def one(o, carry):
            outgoing(kind, lax.rem(me + o, streams)).wait_send()
            return carry

        lax.fori_loop(1, streams, one, 0)

    def keep_own(kind):
        out, into = boxes[kind]
        into[me] = out[me]

    inner = (me > 0) & (me < last)

    @pl.when(inner)
    def _():
        send_some(MAT_F, 0, last)

    def inner_face(f, carry):
        put(flux_stream, (f,), roe_twice(get(prim, (f,), 7), get(prim, (f + 1,), 7), 0))
        return carry

    def span_plane(p, carry):
        cell = get(prim, (p + 1,), 7)
        ahead = [pltpu.roll(field, lanes - 1, 1) for field in cell]
        face = roe_twice(cell, ahead, 2)
        put(res, (p,), [f - pltpu.roll(f, 1, 1) for f in face])
        return carry

    lax.fori_loop(0, planes, span_plane, 0)
    lax.fori_loop(1, planes, inner_face, 0)
    halos[0].wait_recv()
    halos[1].wait_recv()
    below = [jnp.where(me == 0, free_values[k], halo_stream[0, k]) for k in range(5)]
    put(prim, (0,), primitive(below))
    above = [
        jnp.where(me == last, state[k, planes - 1], halo_stream[1, k]) for k in range(5)
    ]
    put(prim, (planes + 1,), primitive(above))
    lax.fori_loop(0, 2, lambda i, c: inner_face(i * planes, c), 0)
    halos[2].wait_recv()
    halos[3].wait_recv()
    loads[2].wait()

    def ghost(cell, kinds):
        out = []
        for k in range(5):
            mirror = -cell[k] if k == 2 else cell[k]
            out.append(
                jnp.where(kinds == 0, mirror, jnp.where(kinds == 1, cell[k], free_values[k]))
            )
        return out

    row_first = [edge[0, k] for k in range(5)]
    row_last = [edge[1, k] for k in range(5)]
    ghost_low = ghost(row_first, kinds[...] & 3)
    ghost_high = ghost(row_last, kinds[...] >> 2)
    side_low = [jnp.where(mine == 0, ghost_low[k], halo_cross[0, k]) for k in range(5)]
    side_high = [
        jnp.where(mine == crosses - 1, ghost_high[k], halo_cross[1, k]) for k in range(5)
    ]
    put(low_prim, (), primitive(side_low))
    put(top_flux, (), roe_twice(primitive(row_last), primitive(side_high), 1))

    row_no = lax.broadcasted_iota(jnp.int32, (rows, lanes), 0)

    def plane_residual(p, carry):
        cell = get(prim, (p + 1,), 7)
        under = [
            jnp.where(row_no == 0, low_prim[k, pl.ds(p, 1), :], pltpu.roll(cell[k], 1, 0))
            for k in range(7)
        ]
        face = roe_twice(under, cell, 1)
        for k in range(5):
            over = jnp.where(
                row_no == rows - 1,
                top_flux[k, pl.ds(p, 1), :],
                pltpu.roll(face[k], rows - 1, 0),
            )
            res[k, p] = 0.5 * (
                (flux_stream[k, p + 1] - flux_stream[k, p]) + (over - face[k]) + res[k, p]
            )
        return carry

    lax.fori_loop(0, planes, plane_residual, 0)
    def plane_drive(p, previous):
        term = half_apply(half_jacobian(get(prim, (p,), 7)), previous, 1.0)
        out = mat_vec(lambda e: diag[e, p], [term[k] - res[k, p] for k in range(5)])
        put(drive, (p,), out)
        return tuple(out)

    current = mat_vec(lambda e: diag[e, 0], [-res[k, 0] for k in range(5)])
    put(drive, (0,), current)
    current = lax.fori_loop(1, planes, plane_drive, tuple(current))
    current = half_apply(half_jacobian(get(prim, (planes,), 7)), current, 1.0)
    for k in range(5):
        pack(a_out, k, current[k])

    @pl.when(me < last)
    def _():
        send_some(VEC_F, 0, last)

    keep_own(MAT_F)
    keep_own(VEC_F)
    lax.fori_loop(0, planes - 1, matrices_b, 0)
    lax.fori_loop(0, 5, product_b, 0)

    def back_down(column, current):
        for p in reversed(range(planes - 1)):
            step = mat_vec(lambda e: mats_b[e, p], current)
            current = [column(k, p) + step[k] for k in range(5)]
        return half_apply(half_jacobian(get(prim, (1,), 7)), current, -1.0)

    for k, value in enumerate(
        back_down(lambda k, p: drive[k, p], get(drive, (planes - 1,), 5))
    ):
        back[25 + k] = value

    def back_column(j, carry):
        delta = [diag[5 * k + j, 0] for k in range(5)]
        put(base, (0,), delta)
        for p in range(1, planes):
            delta = mat_vec(lambda e: mats_f[e, p], delta)
            put(base, (p,), delta)
        for r, value in enumerate(back_down(lambda k, p: base[k, p], delta)):
            back[5 * r + j] = value
        return carry

    lax.fori_loop(0, 5, back_column, 0)
    keep_own(MAT_B)
    half = streams // 2

    @pl.when(inner)
    def _():
        sent(MAT_F)
        send_some(MAT_B, 0, half - 1)

    def hand_back(kind, to, values):
        out, into = boxes[kind]
        for k in range(5):
            out[to, k] = values[k]

        @pl.when(to != me)
        def _():
            outgoing(kind, to).start()

        @pl.when(to == me)
        def _():
            for k in range(5):
                into[me, k] = values[k]

    wait_from(VEC_F, 0)
    current = [a_in[0, k] for k in range(5)]
    hand_back(BACK_F, 1, current)

    def scan_f(j, vec):
        wait_from(MAT_F, j)
        wait_from(VEC_F, j)
        step = mat_vec(lambda e: p_in[j, e], vec)
        out = [a_in[j, k] + step[k] for k in range(5)]
        hand_back(BACK_F, j + 1, out)
        return tuple(out)

    lax.fori_loop(1, last, scan_f, tuple(current))

    @pl.when(inner)
    def _():
        send_some(MAT_B, half - 1, last)

    def gather(kind):
        def one(j, carry):
            wait_from(kind, j)
            return carry

        lax.fori_loop(0, streams, one, 0)

    def joined(into, k):
        wide = []
        for c in range(chunks):
            parts = [into[c * per_chunk + i, k] for i in range(per_chunk)]
            wide.append(parts[0] if per_chunk == 1 else jnp.concatenate(parts, axis=0))
        return wide[0] if chunks == 1 else jnp.concatenate(wide, axis=1)

    @pl.when(me > 0)
    def _():
        gather(BACK_F)

    incoming = [jnp.where(me == 0, 0.0, joined(s_in, k)) for k in range(5)]
    step = mat_vec(lambda e: back[e], incoming)
    for k in range(5):
        pack(b_out, k, back[25 + k] + step[k])

    @pl.when(me > 0)
    def _():
        send_some(VEC_B, 0, last)

    keep_own(VEC_B)
    delta = incoming
    for p in range(planes):
        delta = mat_vec(lambda e: diag[e, 0] if p == 0 else mats_f[e, p], delta)
        current = [drive[k, p] + delta[k] for k in range(5)]
        put(base, (p,), current)
    for p in reversed(range(planes - 1)):
        step = mat_vec(lambda e: mats_b[e, p], current)
        current = [base[k, p] + step[k] for k in range(5)]
        put(base, (p,), current)

    wait_from(VEC_B, last)
    current = [b_in[last, k] for k in range(5)]
    hand_back(BACK_B, last - 1, current)

    def scan_b(n, vec):
        j = last - n
        wait_from(MAT_B, j)
        wait_from(VEC_B, j)
        step = mat_vec(lambda e: q_in[j, e], vec)
        out = [b_in[j, k] + step[k] for k in range(5)]
        hand_back(BACK_B, j - 1, out)
        return tuple(out)

    lax.fori_loop(1, last, scan_b, tuple(current))

    @pl.when(me < last)
    def _():
        gather(BACK_B)

    delta = [jnp.where(me == last, 0.0, joined(u_in, k)) for k in range(5)]
    for p in reversed(range(planes)):
        if p == planes - 1:
            delta = [-d for d in mat_vec(lambda e: diag[e, p], delta)]
        else:
            delta = mat_vec(lambda e: mats_b[e, p], delta)
        for k in range(5):
            upd[k, p] = base[k, p] + delta[k]

    for copy in halos:
        copy.wait_send()

    @pl.when(inner)
    def _():
        sent(MAT_B)

    @pl.when(me < last)
    def _():
        sent(VEC_F)

    @pl.when(me > 0)
    def _():
        sent(VEC_B)

    def sent_back(t, carry):
        @pl.when(t != me)
        def _():
            outgoing(BACK_F, t).wait_send()

        @pl.when(t - 1 != me)
        def _():
            outgoing(BACK_B, t - 1).wait_send()

        return carry

    lax.fori_loop(1, streams, sent_back, 0)


def store(res, upd, res_out, upd_out, sem):
    copies = [
        pltpu.make_async_copy(src, dst, sem.at[i])
        for i, (src, dst) in enumerate([(res, res_out), (upd, upd_out)])
    ]
    for copy in copies:
        copy.start()
    for copy in copies:
        copy.wait()


def local(streams, crosses, state, diag, kinds_low, kinds_high):
    _, planes, rows, lanes = state.shape
    piece = rows * (lanes // CHUNK) // streams
    f32 = jnp.float32
    block = (planes, rows, lanes)

    def vmem(*shape):
        return pltpu.VMEM(shape, f32)

    residual, update = pl.pallas_call(
        functools.partial(kernel, streams, crosses),
        out_shape=[jax.ShapeDtypeStruct(state.shape, f32)] * 2,
        in_specs=[pl.BlockSpec(memory_space=pltpu.HBM)] * 3,
        out_specs=[pl.BlockSpec(memory_space=pltpu.VMEM)] * 2,
        scratch_shapes=[
            vmem(5, *block),
            vmem(25, *block),
            pltpu.VMEM((planes, lanes), jnp.int32),
            vmem(7, planes + 2, rows, lanes),
            vmem(2, 5, planes, lanes),
            vmem(2, 5, planes, lanes),
            vmem(2, 5, rows, lanes),
            vmem(7, planes, lanes),
            vmem(5, planes, lanes),
            vmem(5, planes + 1, rows, lanes),
            vmem(5, *block),
            vmem(25, *block),
            vmem(25, *block),
            vmem(5, *block),
            vmem(30, rows, lanes),
            *[vmem(streams, 25, piece, CHUNK)] * 4,
            *[vmem(streams, 5, piece, CHUNK)] * 8,
            pltpu.SemaphoreType.DMA((3,)),
            pltpu.SemaphoreType.DMA((4,)),
            pltpu.SemaphoreType.DMA((4,)),
            pltpu.SemaphoreType.DMA((6, streams)),
            pltpu.SemaphoreType.DMA((6, streams)),
        ],
        compiler_params=pltpu.CompilerParams(
            collective_id=0, has_side_effects=True, vmem_limit_bytes=54400 * 1024
        ),
        cost_estimate=pl.CostEstimate(
            flops=16000000, bytes_accessed=2700000, transcendentals=100000
        ),
    )(state, diag, kinds_low + 4 * kinds_high)
    return pl.pallas_call(
        store,
        out_shape=[jax.ShapeDtypeStruct(state.shape, f32)] * 2,
        in_specs=[pl.BlockSpec(memory_space=pl.ANY)] * 2,
        out_specs=[pl.BlockSpec(memory_space=pl.ANY)] * 2,
        scratch_shapes=[pltpu.SemaphoreType.DMA((2,))],
        cost_estimate=pl.CostEstimate(flops=0, bytes_accessed=1310720, transcendentals=0),
    )(residual, update)


def solution(mesh):
    spec = P(None, "stream", "cross", None)
    return jax.shard_map(
        functools.partial(local, mesh.shape["stream"], mesh.shape["cross"]),
        mesh=mesh,
        in_specs=(spec, spec, P("stream", None), P("stream", None)),
        out_specs=(spec, spec),
        check_vma=False,
    )
```

```python
import functools

import jax
import jax.numpy as jnp
from jax import lax
from jax.experimental import pallas as pl
from jax.experimental.pallas import tpu as pltpu
from jax.sharding import PartitionSpec as P

MESH = pl.DeviceIdType.MESH
free_values = (1.0, 0.0, 0.0, 0.0, 2.5)
CHUNK = 128
RHO, U1, U2, U3, PRES, ENTH, ROOT = range(7)


def primitive(q):
    inv_root = lax.rsqrt(q[0])
    inv = inv_root * inv_root
    u = [q[1] * inv, q[2] * inv, q[3] * inv]
    pressure = 0.4 * (q[4] - 0.5 * (q[1] * u[0] + q[2] * u[1] + q[3] * u[2]))
    return [q[0], *u, pressure, (q[4] + pressure) * inv, q[0] * inv_root]


def roe_twice(left, right, d):
    share = right[ROOT] / (left[ROOT] + right[ROOT])
    jump = [right[1 + k] - left[1 + k] for k in range(3)]
    avg = [left[1 + k] + share * jump[k] for k in range(3)]
    enth = left[ENTH] + share * (right[ENTH] - left[ENTH])
    kinetic = 0.5 * (avg[0] * avg[0] + avg[1] * avg[1] + avg[2] * avg[2])
    sound_sq = 0.4 * (enth - kinetic)
    inv_sound = lax.rsqrt(sound_sq)
    sound = sound_sq * inv_sound
    inv_sq = inv_sound * inv_sound
    dens = left[ROOT] * right[ROOT]
    normal = avg[d]
    scaled_pres = (right[PRES] - left[PRES]) * inv_sq
    scaled_jump = dens * inv_sound * jump[d]
    slow = jnp.abs(normal - sound) * (0.5 * (scaled_pres - scaled_jump))
    fast = jnp.abs(normal + sound) * (0.5 * (scaled_pres + scaled_jump))
    speed = jnp.abs(normal)
    entropy = speed * (right[RHO] - left[RHO] - scaled_pres)
    shear = speed * dens
    acoustic = slow + fast
    total = acoustic + entropy
    spread = (fast - slow) * sound
    mass_left = left[RHO] * left[1 + d]
    mass_right = right[RHO] * right[1 + d]
    pieces = [mass_left + mass_right - total]
    along = 0.0
    for k in range(3):
        central = mass_left * left[1 + k] + mass_right * right[1 + k]
        if k == d:
            pieces.append(central + (left[PRES] + right[PRES]) - (total * avg[k] + spread))
        else:
            pieces.append(central - (total * avg[k] + shear * jump[k]))
            along = along + avg[k] * jump[k]
    pieces.append(
        mass_left * left[ENTH]
        + mass_right * right[ENTH]
        - (acoustic * enth + spread * normal + entropy * kinetic + shear * along)
    )
    return pieces


def half_jacobian(w):
    u, v, s = 0.5 * w[U1], 0.5 * w[U2], 0.5 * w[U3]
    phi = 0.1 * (w[U1] * w[U1] + w[U2] * w[U2] + w[U3] * w[U3])
    inv_root = w[ROOT] / w[RHO]
    pos = 1.4 * w[PRES]
    lam = jnp.abs(u) + 0.5 * (pos * lax.rsqrt(pos) * inv_root)
    return u, v, s, phi, 0.5 * w[ENTH], lam, w[U1], w[U2], w[U3]


def row_times(row, jac, sign):
    u, v, s, phi, enth, lam, u1, _, _ = jac
    pres = row[1] + u1 * row[4]
    move = u * row[1] + v * row[2] + s * row[3] + enth * row[4]
    own = u + sign * lam
    return [
        phi * pres - u1 * move + (sign * lam) * row[0],
        0.5 * row[0] + own * row[1] + move - 0.4 * (u * pres),
        own * row[2] - 0.4 * (v * pres),
        own * row[3] - 0.4 * (s * pres),
        own * row[4] + 0.2 * pres,
    ]


def half_apply(jac, vec, sign):
    u, v, s, phi, enth, lam, u1, _, _ = jac
    own = u + sign * lam
    q = vec[1] - u1 * vec[0]
    pres = phi * vec[0] - 0.4 * (u * vec[1] + v * vec[2] + s * vec[3]) + 0.2 * vec[4]
    return [
        0.5 * vec[1] + (sign * lam) * vec[0],
        own * vec[1] + u * q + pres,
        own * vec[2] + v * q,
        own * vec[3] + s * q,
        own * vec[4] + u1 * pres + enth * q,
    ]


def mat_vec(load, vec):
    out = []
    for r in range(5):
        term = [load(5 * r + k) * vec[k] for k in range(5)]
        out.append((term[0] + term[1]) + (term[2] + term[3]) + term[4])
    return out


def kernel(
    streams, crosses,
    state_hbm, diag_hbm, kinds_hbm, res, upd,
    state, diag, kinds, prim, edge, halo_cross, halo_stream, low_prim, top_flux,
    flux_stream, drive, mats_f, mats_b, base,
    p_out, p_in, q_out, q_in, a_out, a_in, s_out, s_in, b_out, b_in, u_out, u_in,
    load_sem, halo_send, halo_recv, sends, recvs,
):
    me = lax.axis_index("stream")
    mine = lax.axis_index("cross")
    planes, rows, lanes = state.shape[1:]
    chunks = lanes // CHUNK
    piece = rows * chunks // streams
    per_chunk = rows // piece
    last = streams - 1
    up = {"stream": lax.rem(me + 1, streams)}
    down = {"stream": lax.rem(me + last, streams)}
    high = {"cross": lax.rem(mine + 1, crosses)}
    low = {"cross": lax.rem(mine + crosses - 1, crosses)}

    loads = [
        pltpu.make_async_copy(src, dst, load_sem.at[i])
        for i, (src, dst) in enumerate(
            [(state_hbm, state), (diag_hbm, diag), (kinds_hbm, kinds)]
        )
    ]
    for copy in loads:
        copy.start()
    barrier = pltpu.get_barrier_semaphore()

    def greet(o, carry):
        pl.semaphore_signal(
            barrier, inc=1, device_id={"stream": lax.rem(me + o, streams)}, device_id_type=MESH
        )
        return carry

    lax.fori_loop(1, streams, greet, 0)
    for to in (high, low):
        pl.semaphore_signal(barrier, inc=1, device_id=to, device_id_type=MESH)

    def get(ref, index, count):
        return [ref[(k, *index)] for k in range(count)]

    def put(ref, index, values):
        for k, value in enumerate(values):
            ref[(k, *index)] = value

    def pack(out, e, value):
        for c in range(chunks):
            for i in range(per_chunk):
                out[c * per_chunk + i, e] = value[
                    i * piece : (i + 1) * piece, c * CHUNK : (c + 1) * CHUNK
                ]

    def matrices_f(p, carry):
        jac = half_jacobian(get(prim, (p,), 7))
        for r in range(5):
            row = [diag[5 * r + k, p] for k in range(5)]
            for k, value in enumerate(row_times(row, jac, 1.0)):
                mats_f[5 * r + k, p] = value
        return carry

    def matrices_b(p, carry):
        jac = half_jacobian(get(prim, (p + 2,), 7))
        for r in range(5):
            row = [-diag[5 * r + k, p] for k in range(5)]
            for k, value in enumerate(row_times(row, jac, -1.0)):
                mats_b[5 * r + k, p] = value
        return carry

    def product_f(j, carry):
        vec = [diag[5 * k + j, 0] for k in range(5)]
        for p in range(1, planes):
            vec = mat_vec(lambda e: mats_f[e, p], vec)
        vec = half_apply(half_jacobian(get(prim, (planes,), 7)), vec, 1.0)
        for r in range(5):
            pack(p_out, 5 * r + j, vec[r])
        return carry

    def product_b(j, carry):
        vec = [-diag[5 * k + j, planes - 1] for k in range(5)]
        for p in reversed(range(planes - 1)):
            vec = mat_vec(lambda e: mats_b[e, p], vec)
        vec = half_apply(half_jacobian(get(prim, (1,), 7)), vec, -1.0)
        for r in range(5):
            pack(q_out, 5 * r + j, vec[r])
        return carry

    def own_plane(p, carry):
        put(prim, (p + 1,), primitive(get(state, (p,), 5)))
        return carry

    loads[0].wait()
    for p in range(planes):
        for k in range(5):
            edge[0, k, pl.ds(p, 1), :] = state[k, p, pl.ds(0, 1), :]
            edge[1, k, pl.ds(p, 1), :] = state[k, p, pl.ds(rows - 1, 1), :]
    lax.fori_loop(0, planes, own_plane, 0)
    loads[1].wait()
    lax.fori_loop(1, planes, matrices_f, 0)
    lax.fori_loop(0, 5, product_f, 0)
    pl.semaphore_wait(barrier, streams + 1)

    def remote(src, dst, send, recv, to):
        return pltpu.make_async_remote_copy(
            src_ref=src, dst_ref=dst, send_sem=send, recv_sem=recv,
            device_id=to, device_id_type=MESH,
        )

    halos = [
        remote(state.at[:, planes - 1], halo_stream.at[0], halo_send.at[0], halo_recv.at[0], up),
        remote(state.at[:, 0], halo_stream.at[1], halo_send.at[1], halo_recv.at[1], down),
        remote(edge.at[1], halo_cross.at[0], halo_send.at[2], halo_recv.at[2], high),
        remote(edge.at[0], halo_cross.at[1], halo_send.at[3], halo_recv.at[3], low),
    ]
    for copy in halos:
        copy.start()

    boxes = [
        (p_out, p_in), (a_out, a_in), (s_out, s_in), (q_out, q_in), (b_out, b_in), (u_out, u_in)
    ]
    MAT_F, VEC_F, BACK_F, MAT_B, VEC_B, BACK_B = range(6)

    def outgoing(kind, to):
        out, into = boxes[kind]
        return remote(
            out.at[to], into.at[me], sends.at[kind, to], recvs.at[kind, me], {"stream": to}
        )

    def wait_from(kind, source):
        out, into = boxes[kind]

        @pl.when(source != me)
        def _():
            remote(
                out.at[source], into.at[source], sends.at[kind, source],
                recvs.at[kind, source], {"stream": source},
            ).wait_recv()

    def send_some(kind, first, end):
        def one(o, carry):
            outgoing(kind, lax.rem(me + o, streams)).start()
            return carry

        lax.fori_loop(first, end, one, 0)

    def sent(kind):
        def one(o, carry):
            outgoing(kind, lax.rem(me + o, streams)).wait_send()
            return carry

        lax.fori_loop(1, streams, one, 0)

    def keep_own(kind, count):
        out, into = boxes[kind]

        def one(e, carry):
            into[me, e] = out[me, e]
            return carry

        lax.fori_loop(0, count, one, 0)

    inner = (me > 0) & (me < last)

    @pl.when(inner)
    def _():
        send_some(MAT_F, 1, streams)

    def inner_face(f, carry):
        put(flux_stream, (f,), roe_twice(get(prim, (f,), 7), get(prim, (f + 1,), 7), 0))
        return carry

    def span_plane(p, carry):
        cell = get(prim, (p + 1,), 7)
        ahead = [pltpu.roll(field, lanes - 1, 1) for field in cell]
        face = roe_twice(cell, ahead, 2)
        put(res, (p,), [f - pltpu.roll(f, 1, 1) for f in face])
        return carry

    lax.fori_loop(0, planes, span_plane, 0)
    lax.fori_loop(1, planes, inner_face, 0)
    halos[0].wait_recv()
    halos[1].wait_recv()
    below = [jnp.where(me == 0, free_values[k], halo_stream[0, k]) for k in range(5)]
    put(prim, (0,), primitive(below))
    above = [
        jnp.where(me == last, state[k, planes - 1], halo_stream[1, k]) for k in range(5)
    ]
    put(prim, (planes + 1,), primitive(above))
    lax.fori_loop(0, 2, lambda i, c: inner_face(i * planes, c), 0)
    halos[2].wait_recv()
    halos[3].wait_recv()
    loads[2].wait()

    def ghost(cell, kinds):
        out = []
        for k in range(5):
            mirror = -cell[k] if k == 2 else cell[k]
            out.append(
                jnp.where(kinds == 0, mirror, jnp.where(kinds == 1, cell[k], free_values[k]))
            )
        return out

    row_first = [edge[0, k] for k in range(5)]
    row_last = [edge[1, k] for k in range(5)]
    ghost_low = ghost(row_first, kinds[...] & 3)
    ghost_high = ghost(row_last, kinds[...] >> 2)
    side_low = [jnp.where(mine == 0, ghost_low[k], halo_cross[0, k]) for k in range(5)]
    side_high = [
        jnp.where(mine == crosses - 1, ghost_high[k], halo_cross[1, k]) for k in range(5)
    ]
    put(low_prim, (), primitive(side_low))
    put(top_flux, (), roe_twice(primitive(row_last), primitive(side_high), 1))

    row_no = lax.broadcasted_iota(jnp.int32, (rows, lanes), 0)

    def plane_residual(p, carry):
        cell = get(prim, (p + 1,), 7)
        under = [
            jnp.where(row_no == 0, low_prim[k, pl.ds(p, 1), :], pltpu.roll(cell[k], 1, 0))
            for k in range(7)
        ]
        face = roe_twice(under, cell, 1)
        for k in range(5):
            over = jnp.where(
                row_no == rows - 1,
                top_flux[k, pl.ds(p, 1), :],
                pltpu.roll(face[k], rows - 1, 0),
            )
            res[k, p] = 0.5 * (
                (flux_stream[k, p + 1] - flux_stream[k, p]) + (over - face[k]) + res[k, p]
            )
        return carry

    lax.fori_loop(0, planes, plane_residual, 0)
    def plane_drive(p, previous):
        term = half_apply(half_jacobian(get(prim, (p,), 7)), previous, 1.0)
        out = mat_vec(lambda e: diag[e, p], [term[k] - res[k, p] for k in range(5)])
        put(drive, (p,), out)
        return tuple(out)

    current = mat_vec(lambda e: diag[e, 0], [-res[k, 0] for k in range(5)])
    put(drive, (0,), current)
    current = lax.fori_loop(1, planes, plane_drive, tuple(current))
    current = half_apply(half_jacobian(get(prim, (planes,), 7)), current, 1.0)
    for k in range(5):
        pack(a_out, k, current[k])

    @pl.when(me < last)
    def _():
        send_some(VEC_F, 1, streams)

    keep_own(MAT_F, 25)
    keep_own(VEC_F, 5)
    lax.fori_loop(0, planes - 1, matrices_b, 0)
    lax.fori_loop(0, 5, product_b, 0)
    keep_own(MAT_B, 25)

    @pl.when(inner)
    def _():
        sent(MAT_F)
        send_some(MAT_B, 1, streams)

    def hand_back(kind, to, values):
        out, into = boxes[kind]
        for k in range(5):
            out[to, k] = values[k]

        @pl.when(to != me)
        def _():
            outgoing(kind, to).start()

        @pl.when(to == me)
        def _():
            for k in range(5):
                into[me, k] = values[k]

    wait_from(VEC_F, 0)
    current = [a_in[0, k] for k in range(5)]
    hand_back(BACK_F, 1, current)

    def scan_f(j, vec):
        wait_from(MAT_F, j)
        wait_from(VEC_F, j)
        step = mat_vec(lambda e: p_in[j, e], vec)
        out = [a_in[j, k] + step[k] for k in range(5)]
        hand_back(BACK_F, j + 1, out)
        return tuple(out)

    lax.fori_loop(1, last, scan_f, tuple(current))

    def gather(kind):
        def one(j, carry):
            wait_from(kind, j)
            return carry

        lax.fori_loop(0, streams, one, 0)

    def joined(into, k):
        wide = []
        for c in range(chunks):
            parts = [into[c * per_chunk + i, k] for i in range(per_chunk)]
            wide.append(parts[0] if per_chunk == 1 else jnp.concatenate(parts, axis=0))
        return wide[0] if chunks == 1 else jnp.concatenate(wide, axis=1)

    @pl.when(me > 0)
    def _():
        gather(BACK_F)

    delta = [jnp.where(me == 0, 0.0, joined(s_in, k)) for k in range(5)]
    for p in range(planes):
        delta = mat_vec(lambda e: diag[e, 0] if p == 0 else mats_f[e, p], delta)
        current = [drive[k, p] + delta[k] for k in range(5)]
        put(base, (p,), current)
    for p in reversed(range(planes - 1)):
        step = mat_vec(lambda e: mats_b[e, p], current)
        current = [base[k, p] + step[k] for k in range(5)]
        put(base, (p,), current)
    current = half_apply(half_jacobian(get(prim, (1,), 7)), current, -1.0)
    for k in range(5):
        pack(b_out, k, current[k])

    @pl.when(me > 0)
    def _():
        send_some(VEC_B, 1, streams)

    keep_own(VEC_B, 5)

    wait_from(VEC_B, last)
    current = [b_in[last, k] for k in range(5)]
    hand_back(BACK_B, last - 1, current)

    def scan_b(n, vec):
        j = last - n
        wait_from(MAT_B, j)
        wait_from(VEC_B, j)
        step = mat_vec(lambda e: q_in[j, e], vec)
        out = [b_in[j, k] + step[k] for k in range(5)]
        hand_back(BACK_B, j - 1, out)
        return tuple(out)

    lax.fori_loop(1, last, scan_b, tuple(current))

    @pl.when(me < last)
    def _():
        gather(BACK_B)

    delta = [jnp.where(me == last, 0.0, joined(u_in, k)) for k in range(5)]
    for p in reversed(range(planes)):
        if p == planes - 1:
            delta = [-d for d in mat_vec(lambda e: diag[e, p], delta)]
        else:
            delta = mat_vec(lambda e: mats_b[e, p], delta)
        for k in range(5):
            upd[k, p] = base[k, p] + delta[k]

    for copy in halos:
        copy.wait_send()

    @pl.when(inner)
    def _():
        sent(MAT_B)

    @pl.when(me < last)
    def _():
        sent(VEC_F)

    @pl.when(me > 0)
    def _():
        sent(VEC_B)

    def sent_back(t, carry):
        @pl.when(t != me)
        def _():
            outgoing(BACK_F, t).wait_send()

        @pl.when(t - 1 != me)
        def _():
            outgoing(BACK_B, t - 1).wait_send()

        return carry

    lax.fori_loop(1, streams, sent_back, 0)


def local(streams, crosses, state, diag, kinds_low, kinds_high):
    _, planes, rows, lanes = state.shape
    piece = rows * (lanes // CHUNK) // streams
    f32 = jnp.float32
    block = (planes, rows, lanes)

    def vmem(*shape):
        return pltpu.VMEM(shape, f32)

    return pl.pallas_call(
        functools.partial(kernel, streams, crosses),
        out_shape=[jax.ShapeDtypeStruct(state.shape, f32)] * 2,
        in_specs=[pl.BlockSpec(memory_space=pltpu.HBM)] * 3,
        out_specs=[pl.BlockSpec(memory_space=pltpu.VMEM)] * 2,
        scratch_shapes=[
            vmem(5, *block),
            vmem(25, *block),
            pltpu.VMEM((planes, lanes), jnp.int32),
            vmem(7, planes + 2, rows, lanes),
            vmem(2, 5, planes, lanes),
            vmem(2, 5, planes, lanes),
            vmem(2, 5, rows, lanes),
            vmem(7, planes, lanes),
            vmem(5, planes, lanes),
            vmem(5, planes + 1, rows, lanes),
            vmem(5, *block),
            vmem(25, *block),
            vmem(25, *block),
            vmem(5, *block),
            *[vmem(streams, 25, piece, CHUNK)] * 4,
            *[vmem(streams, 5, piece, CHUNK)] * 8,
            pltpu.SemaphoreType.DMA((3,)),
            pltpu.SemaphoreType.DMA((4,)),
            pltpu.SemaphoreType.DMA((4,)),
            pltpu.SemaphoreType.DMA((6, streams)),
            pltpu.SemaphoreType.DMA((6, streams)),
        ],
        compiler_params=pltpu.CompilerParams(
            collective_id=0, has_side_effects=True, vmem_limit_bytes=54400 * 1024
        ),
        cost_estimate=pl.CostEstimate(
            flops=16000000, bytes_accessed=2700000, transcendentals=100000
        ),
    )(state, diag, kinds_low + 4 * kinds_high)


def solution(mesh):
    spec = P(None, "stream", "cross", None)
    return jax.shard_map(
        functools.partial(local, mesh.shape["stream"], mesh.shape["cross"]),
        mesh=mesh,
        in_specs=(spec, spec, P("stream", None), P("stream", None)),
        out_specs=(spec, spec),
        check_vma=False,
    )
```
